32 devices in a mesh: gz: 8 (over y, x, core), ch: 4 (over z).
Axes of the slice: x: 2, y: 2, z: 4, core: 2. Of those that a mesh axis runs over, the one named last changes fastest.
Arguments:
- inputs: bfloat16 [16, 32, 6144], P('gz', 'ch'), may hold values from -6 to 6
- out_grad: bfloat16 [16, 32, 6144], P('gz', 'ch'), may hold values from -6 to 6
- filters: bfloat16 [864, 32], replicated, may hold values from -0.21875 to 0.21875
Outputs:
- in_grad: bfloat16 [16, 32, 6144], P('gz', 'ch')
- filter_grad: float32 [864, 32], replicated
The draws below stay inside these ranges and needn't reach their ends.
All inputs are finite; a program needn't handle non-finite values.
Results may differ from the reference program's by a relative error of at most 0.001.
Values may be sent and summed in bfloat16 or wider, within the bound.
No kernel may reach another device: no remote copies, remote signals or barrier semaphores. Data moves between devices by JAX's collectives and lax.ppermute only.
A program may use at most 64 MiB of HBM per device.

```python
import jax
import jax.numpy as jnp
from jax import lax

CH = 32
NX = 192
NZ = 16
NY = 32
CELLS = 98304


def shard_levels(key, dims, pieces, low, largest):
    def one(dim, parts):
        draws = jax.random.uniform(jax.random.fold_in(jax.random.fold_in(key, 6), dim), (parts,), jnp.float32, low / len(pieces), largest / len(pieces))
        return jnp.repeat(jnp.exp(draws), dims[dim] // parts).reshape((-1,) + (1,) * (len(dims) - dim - 1))

    level = one(*pieces[0])
    for cut in pieces[1:]:
        level = level * one(*cut)
    return level


def gaussian(own_key, shape, width, reach, pieces=(), kind=jnp.bfloat16):
    result = width * jax.random.normal(own_key, shape, jnp.float32)
    if pieces:
        result = result * shard_levels(own_key, shape, pieces, -0.22, 0.18)
    return jnp.clip(result, -reach, reach).astype(kind)


def setup_inputs(seed: int = 0) -> dict:
    keys = jax.random.split(jax.random.key(seed), 4)
    inputs = gaussian(keys[0], (NZ, NY, NX * CH), 1.0, 6.0, ((0, 8), (1, 4)))
    out_grad = gaussian(keys[1], (NZ, NY, NX * CH), 1.0, 6.0, ((0, 8), (1, 4)))
    filters = gaussian(keys[2], (27 * CH, CH), (27 * CH) ** -0.5, 0.21875)
    return {"inputs": inputs, "out_grad": out_grad, "filters": filters}


def forward(values, kernel):
    padded = jnp.pad(values, ((0, 0), (1, 1), (1, 1), (1, 1), (0, 0)), mode='wrap')
    return lax.conv_general_dilated(padded, kernel, (1, 1, 1), 'VALID', dimension_numbers=('NDHWC', 'DHWIO', 'NDHWC'), precision=lax.Precision.HIGHEST)

def reference(inputs, out_grad, filters):
    values = inputs.astype(jnp.float32).reshape(1, NZ, NY, NX, CH)
    kernel = filters.astype(jnp.float32).reshape(3, 3, 3, CH, CH)
    upstream = out_grad.astype(jnp.float32).reshape(1, NZ, NY, NX, CH)
    outputs, pullback = jax.vjp(forward, values, kernel)
    grad_values, grad_kernel = pullback(upstream)
    in_grad = grad_values.reshape(NZ, NY, NX * CH).astype(jnp.bfloat16)
    scale = jnp.float32(1.0) / jnp.sqrt(jnp.float32(CELLS))
    filter_grad = grad_kernel.reshape(27 * CH, CH).astype(jnp.float32) * scale
    return (in_grad, filter_grad)
```

```python
import functools

import jax
import jax.numpy as jnp
from jax import lax
from jax.experimental import pallas as pl
from jax.experimental.pallas import tpu as pltpu
from jax.sharding import PartitionSpec as P

LANES = 128
TAPS = 3
ORDER = (0, 2, 1)
F32 = jnp.float32
BF16 = jnp.bfloat16


def windows(layer):
    width = layer.shape[1]
    moved = pltpu.roll(layer, LANES // 2, axis=1)
    tiles = [moved[:, at : at + LANES] for at in range(0, width, LANES)]
    left = jnp.concatenate(tiles, axis=0)
    right = jnp.concatenate(tiles[1:] + tiles[:1], axis=0)
    return jnp.concatenate([left, right], axis=1).astype(BF16)


def stacked(layer):
    return jnp.concatenate(
        [layer[:, at : at + LANES] for at in range(0, layer.shape[1], LANES)], axis=0
    )


def prep_kernel(og_ref, f_ref, e_ref, w_ref):
    depth = og_ref.shape[0]
    chans = f_ref.shape[1]
    cells = LANES // chans
    for z in range(depth):
        e_ref[z] = windows(og_ref[z].astype(F32))
    filters = f_ref[...]
    source = lax.broadcasted_iota(jnp.int32, (chans, 2 * LANES), 0)
    target = lax.broadcasted_iota(jnp.int32, (chans, 2 * LANES), 1)
    placed = {}
    for spot in range(1, cells + 3):
        choose = jnp.where(target == source + spot * chans, 1.0, 0.0).astype(BF16)
        placed[spot] = jnp.dot(filters, choose, preferred_element_type=F32)
    for kz in range(TAPS):
        for slot, ky in enumerate(ORDER):
            for b in range(cells):
                total = None
                for kx in range(TAPS):
                    row = ((kz * TAPS + ky) * TAPS + kx) * chans
                    part = placed[b - kx + 3][row : row + chans]
                    total = part if total is None else total + part
                at = slot * LANES + b * chans
                w_ref[kz, at : at + chans] = total.astype(BF16)


def filter_kernel(
    flag_ref, in_ref, lo_ref, hi_ref, og_ref, below_ref, above_ref, e_ref,
    keep_ref, send_ref, eb_ref, ea_ref, first_ref, second_ref, *, chans
):
    depth, rows, width = in_ref.shape
    cells = LANES // chans
    below = below_ref[...].astype(F32)
    above = above_ref[...].astype(F32)
    wb, wa = windows(below), windows(above)
    eb_ref[...] = wb
    ea_ref[...] = wa
    layers = [below] + [og_ref[z].astype(F32) for z in range(depth)] + [above]
    tops = jnp.concatenate([layer[0:1] for layer in layers], axis=0)
    ends = jnp.concatenate([layer[rows - 1 : rows] for layer in layers], axis=0)
    even = flag_ref[1] == 0
    first_ref[...] = jnp.where(even, ends, tops).astype(BF16)
    second_ref[...] = jnp.where(even, tops, ends).astype(BF16)
    y = lax.broadcasted_iota(jnp.int32, (rows, width), 0)
    lo = lo_ref[...].astype(F32)
    hi = hi_ref[...].astype(F32)
    sides = [[], [], []]
    for z in range(depth):
        own = in_ref[z].astype(F32)
        sides[0].append(stacked(jnp.where(y == 0, lo[z : z + 1], pltpu.roll(own, 1, axis=0))))
        sides[1].append(stacked(own))
        sides[2].append(stacked(jnp.where(y == rows - 1, hi[z : z + 1], pltpu.roll(own, rows - 1, axis=0))))
    values = jnp.concatenate(
        [jnp.concatenate(side, axis=0).astype(BF16) for side in sides], axis=1
    )
    own_e = [e_ref[z] for z in range(depth)]
    every = [wb] + own_e + [wa]
    pairs = []
    for kz in range(TAPS):
        window = jnp.concatenate(every[2 - kz : 2 - kz + depth], axis=0)
        product = lax.dot_general(
            values, window, (((0,), (0,)), ((), ())), preferred_element_type=F32
        )
        for ky in range(TAPS):
            total = None
            for b in range(cells):
                at = ky * LANES + b * chans
                part = pltpu.roll(product[at : at + chans], 2 * LANES - (b + 1) * chans, axis=1)[:, :LANES]
                total = part if total is None else total + part
            pairs.append(total)
    lane = lax.broadcasted_iota(jnp.int32, (chans, LANES), 1)
    valid = TAPS * chans
    full = packed_blocks(chans)
    blocks = []
    for r in range(full):
        extra = jnp.zeros((chans, LANES), F32)
        if r // TAPS + full < TAPS * TAPS:
            extra = pltpu.roll(pairs[full + r // TAPS], (valid - (r % TAPS) * chans) % LANES, axis=1)
        blocks.append(jnp.where(lane < valid, pairs[r], extra))
    half = full * chans // 2
    packed = jnp.concatenate(blocks, axis=0)
    core = flag_ref[0] == 0
    low, high = packed[:half], packed[half:]
    keep_ref[...] = jnp.where(core, low, high)
    send_ref[...] = jnp.where(core, high, low)


def packed_blocks(chans):
    return -(-TAPS * TAPS * TAPS * chans // LANES)


def grad_kernel(e_ref, eb_ref, ea_ref, w_ref, lo_ref, hi_ref, out_ref):
    depth, rows, width = out_ref.shape
    blocks = width // LANES
    every = [eb_ref[...]] + [e_ref[z] for z in range(depth)] + [ea_ref[...]]
    turned = (((1,), (1,)), ((), ()))
    edges = windows(jnp.concatenate([lo_ref[...].astype(F32), hi_ref[...].astype(F32)], axis=0))
    layers = depth + 2
    side = None
    for kz in range(TAPS):
        part = lax.dot_general(edges, w_ref[kz, : 2 * LANES], turned, preferred_element_type=F32)
        part = part.reshape(blocks, 2 * layers, 2 * LANES)
        if kz < 2:
            part = pltpu.roll(part, 2 * layers - (2 - kz), axis=1)
        side = part if side is None else side + part
    y = lax.broadcasted_iota(jnp.int32, (blocks, rows, LANES), 1)
    for z in range(depth):
        total = None
        for kz in range(TAPS):
            part = lax.dot_general(every[z - kz + 2], w_ref[kz], turned, preferred_element_type=F32)
            total = part if total is None else total + part
        total = total.reshape(blocks, rows, TAPS * LANES)
        up, down, centre = (total[:, :, slot * LANES : (slot + 1) * LANES] for slot in range(TAPS))
        from_hi = pltpu.roll(side[:, :, :LANES], (rows - 1 - layers - z) % rows, axis=1)
        from_lo = pltpu.roll(side[:, :, LANES:], (rows - z) % rows, axis=1)
        up = jnp.where(y == rows - 1, from_hi, pltpu.roll(up, rows - 1, axis=1))
        down = jnp.where(y == 0, from_lo, pltpu.roll(down, 1, axis=1))
        result = (centre + up + down).astype(BF16)
        for j in range(blocks):
            out_ref[z, :, j * LANES : (j + 1) * LANES] = result[j]


def final_kernel(flag_ref, own_ref, other_ref, out_ref, *, chans, scale):
    core = flag_ref[0] == 0
    own, other = own_ref[...] * scale, other_ref[...] * scale
    packed = jnp.concatenate([jnp.where(core, own, other), jnp.where(core, other, own)], axis=0)
    full = packed_blocks(chans)
    for pair in range(TAPS * TAPS):
        for kx in range(TAPS):
            place = TAPS - 1 - kx
            if pair < full:
                block, lane = pair, place * chans
            else:
                block, lane = (pair - full) * TAPS + place, TAPS * chans
            piece = packed[block * chans : (block + 1) * chans]
            if lane:
                piece = pltpu.roll(piece, LANES - lane, axis=1)
            row = (pair * TAPS + kx) * chans
            out_ref[row : row + chans] = piece[:, :chans]


def call(kernel, outs, n_in, flag=False, cost=0):
    vmem = pl.BlockSpec(memory_space=pltpu.VMEM)
    ins = [vmem] * n_in
    if flag:
        ins = [pl.BlockSpec(memory_space=pltpu.SMEM)] + ins
    single = len(outs) == 1
    return pl.pallas_call(
        kernel,
        out_shape=outs[0] if single else outs,
        in_specs=ins,
        out_specs=vmem if single else [vmem] * len(outs),
        compiler_params=pltpu.CompilerParams(vmem_limit_bytes=40 * 1024 * 1024),
        cost_estimate=pl.CostEstimate(flops=cost, bytes_accessed=1 << 20, transcendentals=0),
    )


def steps(size):
    rounds, stride = [], 1
    while size > 1:
        factor = next(f for f in range(2, size + 1) if size % f == 0)

        def move(k, stride=stride, factor=factor):
            return lambda p: p + ((p // stride + k) % factor - p // stride % factor) * stride

        rounds.append([move(k) for k in range(1, factor)])
        stride *= factor
        size //= factor
    return rounds


def per_device(inputs, out_grad, filters):
    depth, rows, width = inputs.shape
    chans = filters.shape[1]
    blocks = width // LANES
    nz, ny = lax.axis_size("gz"), lax.axis_size("ch")
    gz, ch = lax.axis_index("gz"), lax.axis_index("ch")
    flag = jnp.stack([gz % 2, ch % 2]).astype(jnp.int32)

    def over(axis, value, move):
        size = lax.axis_size(axis)
        return lax.ppermute(value, axis, [(p, move(p)) for p in range(size)])

    below = over("gz", out_grad[depth - 1], lambda p: (p + 1) % nz)
    above = over("gz", out_grad[0], lambda p: (p - 1) % nz)
    lo = over("ch", inputs[:, rows - 1], lambda p: (p + 1) % ny)
    hi = over("ch", inputs[:, 0], lambda p: (p - 1) % ny)

    wide = jax.ShapeDtypeStruct((blocks * rows, 2 * LANES), BF16)
    e, w = call(
        prep_kernel,
        [
            jax.ShapeDtypeStruct((depth,) + wide.shape, BF16),
            jax.ShapeDtypeStruct((TAPS, TAPS * LANES, 2 * LANES), BF16),
        ],
        2,
        cost=1 << 29,
    )(out_grad, filters)

    half = jax.ShapeDtypeStruct((packed_blocks(chans) * chans // 2, LANES), F32)
    edge = jax.ShapeDtypeStruct((depth + 2, width), BF16)
    keep, send, eb, ea, first, second = call(
        functools.partial(filter_kernel, chans=chans),
        [half, half, wide, wide, edge, edge],
        7,
        flag=True,
        cost=1 << 29,
    )(flag, inputs, lo, hi, out_grad, below, above, e)

    total = keep + over("gz", send, lambda p: p ^ 1)
    line = steps(ny) if ny != 4 else [[lambda p: p ^ 1], [lambda p: 3 - p]]
    rounds = [("ch", moves) for moves in line]
    rounds += [("gz", [lambda p, m=m: m(p // 2) * 2 + p % 2 for m in moves]) for moves in steps(nz // 2)]
    received = {}
    for number, (axis, moves) in enumerate(rounds):
        got = [over(axis, total, move) for move in moves]
        if number == 0:
            received[0] = over("ch", first, lambda p: p ^ 1)
        if number == 1:
            received[1] = over("ch", second, lambda p: ((p ^ 1) + (1 if p % 2 else -1) * 2) % ny)
        for value in got:
            total = total + value
    even = ch % 2 == 0
    from_lo = jnp.where(even, received[1], received[0])
    from_hi = jnp.where(even, received[0], received[1])
    in_grad = call(grad_kernel, [jax.ShapeDtypeStruct(inputs.shape, BF16)], 6, cost=1 << 30)(
        e, eb, ea, w, from_lo, from_hi
    )
    other = over("gz", total, lambda p: p ^ 1)
    count = depth * rows * (width // chans) * nz * ny
    scale = float(1.0 / count**0.5)
    filter_grad = call(
        functools.partial(final_kernel, chans=chans, scale=scale),
        [jax.ShapeDtypeStruct(filters.shape, F32)],
        2,
        flag=True,
    )(flag, total, other)
    return (in_grad, filter_grad)


def solution(mesh):
    placed = (P("gz", "ch", None), P("gz", "ch", None), P())
    return jax.shard_map(
        per_device,
        mesh=mesh,
        in_specs=placed,
        out_specs=(P("gz", "ch", None), P()),
        check_vma=False,
    )
```

```python
import functools

import jax
import jax.numpy as jnp
from jax import lax
from jax.experimental import pallas as pl
from jax.experimental.pallas import tpu as pltpu
from jax.sharding import PartitionSpec as P

LANES = 128
TAPS = 3
ORDER = (0, 2, 1)
F32 = jnp.float32
BF16 = jnp.bfloat16


def windows(layer):
    width = layer.shape[1]
    moved = pltpu.roll(layer, LANES // 2, axis=1)
    tiles = [moved[:, at : at + LANES] for at in range(0, width, LANES)]
    left = jnp.concatenate(tiles, axis=0)
    right = jnp.concatenate(tiles[1:] + tiles[:1], axis=0)
    return jnp.concatenate([left, right], axis=1).astype(BF16)


def stacked(layer):
    return jnp.concatenate(
        [layer[:, at : at + LANES] for at in range(0, layer.shape[1], LANES)], axis=0
    )


def prep_kernel(og_ref, in_ref, f_ref, e_ref, w_ref, t_ref):
    depth, rows = og_ref.shape[:2]
    chans = f_ref.shape[0]
    cells = LANES // chans
    for z in range(depth):
        e_ref[z] = windows(og_ref[z].astype(F32))
    filters = f_ref[...]
    source = lax.broadcasted_iota(jnp.int32, (chans, 2 * LANES), 0)
    target = lax.broadcasted_iota(jnp.int32, (chans, 2 * LANES), 1)
    placed = {}
    for spot in range(1, cells + 3):
        choose = jnp.where(target == source + spot * chans, 1.0, 0.0).astype(BF16)
        placed[spot] = lax.dot_general(
            filters, choose, (((0,), (0,)), ((), ())), preferred_element_type=F32
        )
    for kz in range(TAPS):
        for slot, ky in enumerate(ORDER):
            for b in range(cells):
                total = None
                for kx in range(TAPS):
                    row = ((kz * TAPS + ky) * TAPS + kx) * chans
                    part = placed[b - kx + 3][row : row + chans]
                    total = part if total is None else total + part
                at = slot * LANES + b * chans
                w_ref[kz, at : at + chans] = total.astype(BF16)
    for ky in range(TAPS):
        shifted = [
            stacked(pltpu.roll(in_ref[z].astype(F32), (1 - ky) % rows, axis=0)) for z in range(depth)
        ]
        t_ref[ky * LANES : (ky + 1) * LANES] = jnp.concatenate(shifted, axis=0).astype(BF16).T


def diagonal(product, chans):
    cells = LANES // chans
    lane = lax.broadcasted_iota(jnp.int32, (chans, LANES), 1)
    total = product[(cells - 1) * chans :, LANES:]
    for b in range(cells - 1):
        part = product[b * chans : (b + 1) * chans]
        part = jnp.where(lane >= (b + 1) * chans, part[:, :LANES], part[:, LANES:])
        total = total + pltpu.roll(part, LANES - (b + 1) * chans, axis=1)
    return total


def filter_kernel(
    flag_ref, t_ref, rowa_ref, rowb_ref, og_ref, layera_ref, layerb_ref, e_ref,
    keep_ref, send_ref, eb_ref, ea_ref, first_ref, second_ref, *, chans
):
    depth, rows, width = og_ref.shape
    core, even = flag_ref[0] == 0, flag_ref[1] == 0
    layera, layerb = layera_ref[...].astype(F32), layerb_ref[...].astype(F32)
    below, above = jnp.where(core, layerb, layera), jnp.where(core, layera, layerb)
    wb, wa = windows(below), windows(above)
    eb_ref[...] = wb
    ea_ref[...] = wa
    layers = [below] + [og_ref[z].astype(F32) for z in range(depth)] + [above]
    tops = jnp.concatenate([layer[0:1] for layer in layers], axis=0)
    ends = jnp.concatenate([layer[rows - 1 : rows] for layer in layers], axis=0)
    first_ref[...] = jnp.where(even, ends, tops).astype(BF16)
    second_ref[...] = jnp.where(even, tops, ends).astype(BF16)
    y = lax.broadcasted_iota(jnp.int32, (rows, width), 0)
    rowa, rowb = rowa_ref[...].astype(F32), rowb_ref[...].astype(F32)
    lo, hi = jnp.where(even, rowb, rowa), jnp.where(even, rowa, rowb)
    edge = [stacked(jnp.where(y == 0, lo[z : z + 1], hi[z : z + 1])) for z in range(depth)]
    edge = jnp.concatenate(edge, axis=0).astype(BF16).T
    lane = lax.broadcasted_iota(jnp.int32, edge.shape, 1) % rows
    values = jnp.concatenate(
        [
            jnp.where(lane == 0, edge, t_ref[:LANES]),
            t_ref[LANES : 2 * LANES],
            jnp.where(lane == rows - 1, edge, t_ref[2 * LANES :]),
        ],
        axis=0,
    )
    own_e = [e_ref[z] for z in range(depth)]
    every = [wb] + own_e + [wa]
    pairs = []
    for kz in range(TAPS):
        window = jnp.concatenate(every[2 - kz : 2 - kz + depth], axis=0)
        product = jnp.dot(values, window, preferred_element_type=F32)
        for ky in range(TAPS):
            total = diagonal(product[ky * LANES : (ky + 1) * LANES], chans)
            pairs.append(total)
    lane = lax.broadcasted_iota(jnp.int32, (chans, LANES), 1)
    valid = TAPS * chans
    full = packed_blocks(chans)
    blocks = []
    for r in range(full):
        extra = jnp.zeros((chans, LANES), F32)
        if r // TAPS + full < TAPS * TAPS:
            extra = pltpu.roll(pairs[full + r // TAPS], (valid - (r % TAPS) * chans) % LANES, axis=1)
        blocks.append(jnp.where(lane < valid, pairs[r], extra))
    half = full * chans // 2
    packed = jnp.concatenate(blocks, axis=0)
    low, high = packed[:half], packed[half:]
    keep_ref[...] = jnp.where(core, low, high)
    send_ref[...] = jnp.where(core, high, low)


def packed_blocks(chans):
    return -(-TAPS * TAPS * TAPS * chans // LANES)


def grad_kernel(e_ref, eb_ref, ea_ref, w_ref, lo_ref, hi_ref, out_ref):
    depth, rows, width = out_ref.shape
    blocks = width // LANES
    every = [eb_ref[...]] + [e_ref[z] for z in range(depth)] + [ea_ref[...]]
    turned = (((1,), (1,)), ((), ()))
    edges = windows(jnp.concatenate([lo_ref[...].astype(F32), hi_ref[...].astype(F32)], axis=0))
    layers = depth + 2
    side = None
    for kz in range(TAPS):
        part = lax.dot_general(edges, w_ref[kz, : 2 * LANES], turned, preferred_element_type=F32)
        part = part.reshape(blocks, 2 * layers, 2 * LANES)
        if kz < 2:
            part = pltpu.roll(part, 2 * layers - (2 - kz), axis=1)
        side = part if side is None else side + part
    y = lax.broadcasted_iota(jnp.int32, (blocks, rows, LANES), 1)
    for z in range(depth):
        total = None
        for kz in range(TAPS):
            part = lax.dot_general(every[z - kz + 2], w_ref[kz], turned, preferred_element_type=F32)
            total = part if total is None else total + part
        total = total.reshape(blocks, rows, TAPS * LANES)
        up, down, centre = (total[:, :, slot * LANES : (slot + 1) * LANES] for slot in range(TAPS))
        from_hi = pltpu.roll(side[:, :, :LANES], (rows - 1 - layers - z) % rows, axis=1)
        from_lo = pltpu.roll(side[:, :, LANES:], (rows - z) % rows, axis=1)
        up = jnp.where(y == rows - 1, from_hi, pltpu.roll(up, rows - 1, axis=1))
        down = jnp.where(y == 0, from_lo, pltpu.roll(down, 1, axis=1))
        result = (centre + up + down).astype(BF16)
        for j in range(blocks):
            out_ref[z, :, j * LANES : (j + 1) * LANES] = result[j]


def final_kernel(flag_ref, own_ref, other_ref, out_ref, *, chans, scale):
    core = flag_ref[0] == 0
    own, other = own_ref[...] * scale, other_ref[...] * scale
    packed = jnp.concatenate([jnp.where(core, own, other), jnp.where(core, other, own)], axis=0)
    turned = packed.T
    full = packed_blocks(chans)
    for pair in range(TAPS * TAPS):
        for kx in range(TAPS):
            place = TAPS - 1 - kx
            if pair < full:
                block = pair
            else:
                block, place = (pair - full) * TAPS + place, TAPS
            at = (pair * TAPS + kx) * chans
            out_ref[:, at : at + chans] = turned[
                place * chans : (place + 1) * chans, block * chans : (block + 1) * chans
            ]


def call(kernel, outs, n_in, flag=False, cost=0):
    vmem = pl.BlockSpec(memory_space=pltpu.VMEM)
    ins = [vmem] * n_in
    if flag:
        ins = [pl.BlockSpec(memory_space=pltpu.SMEM)] + ins
    single = len(outs) == 1
    return pl.pallas_call(
        kernel,
        out_shape=outs[0] if single else outs,
        in_specs=ins,
        out_specs=vmem if single else [vmem] * len(outs),
        compiler_params=pltpu.CompilerParams(vmem_limit_bytes=40 * 1024 * 1024),
        cost_estimate=pl.CostEstimate(flops=cost, bytes_accessed=1 << 20, transcendentals=0),
    )


def steps(size):
    rounds, stride = [], 1
    while size > 1:
        factor = next(f for f in range(2, size + 1) if size % f == 0)

        def move(k, stride=stride, factor=factor):
            return lambda p: p + ((p // stride + k) % factor - p // stride % factor) * stride

        rounds.append([move(k) for k in range(1, factor)])
        stride *= factor
        size //= factor
    return rounds


def per_device(inputs, out_grad, filters):
    depth, rows, width = inputs.shape
    chans = filters.shape[1]
    blocks = width // LANES
    nz, ny = lax.axis_size("gz"), lax.axis_size("ch")
    gz, ch = lax.axis_index("gz"), lax.axis_index("ch")
    flag = jnp.stack([gz % 2, ch % 2]).astype(jnp.int32)

    def over(axis, value, move):
        size = lax.axis_size(axis)
        return lax.ppermute(value, axis, [(p, move(p)) for p in range(size)])

    core, even = gz % 2 == 0, ch % 2 == 0
    here = lambda p: p ^ 1
    there = lambda n: lambda p: (p + (1 if p % 2 else -1)) % n
    layerb = over("gz", jnp.where(core, out_grad[0], out_grad[depth - 1]), there(nz))
    layera = over("gz", jnp.where(core, out_grad[depth - 1], out_grad[0]), here)
    rowb = over("ch", jnp.where(even, inputs[:, 0], inputs[:, rows - 1]), there(ny))
    rowa = over("ch", jnp.where(even, inputs[:, rows - 1], inputs[:, 0]), here)

    wide = jax.ShapeDtypeStruct((blocks * rows, 2 * LANES), BF16)
    e, w, turned = call(
        prep_kernel,
        [
            jax.ShapeDtypeStruct((depth,) + wide.shape, BF16),
            jax.ShapeDtypeStruct((TAPS, TAPS * LANES, 2 * LANES), BF16),
            jax.ShapeDtypeStruct((TAPS * LANES, depth * blocks * rows), BF16),
        ],
        3,
        cost=1 << 29,
    )(out_grad, inputs, filters.T)

    half = jax.ShapeDtypeStruct((packed_blocks(chans) * chans // 2, LANES), F32)
    edge = jax.ShapeDtypeStruct((depth + 2, width), BF16)
    keep, send, eb, ea, first, second = call(
        functools.partial(filter_kernel, chans=chans),
        [half, half, wide, wide, edge, edge],
        7,
        flag=True,
        cost=1 << 29,
    )(flag, turned, rowa, rowb, out_grad, layera, layerb, e)

    total = keep + over("gz", send, here)
    rounds = [("gz", [lambda p, m=m: m(p // 2) * 2 + p % 2 for m in moves]) for moves in steps(nz // 2)]
    rounds += [("ch", moves) for moves in steps(ny)]
    recva, recvb = over("ch", first, here), over("ch", second, there(ny))
    from_lo = jnp.where(even, recvb, recva)
    from_hi = jnp.where(even, recva, recvb)
    for number, (axis, moves) in enumerate(rounds):
        got = [over(axis, total, move) for move in moves]
        for value in got:
            total = total + value
        if number == len(rounds) - 1:
            in_grad = call(grad_kernel, [jax.ShapeDtypeStruct(inputs.shape, BF16)], 6, cost=1 << 30)(
                e, eb, ea, w, from_lo, from_hi
            )
            total, in_grad = lax.optimization_barrier((total, in_grad))
    other = over("gz", total, here)
    count = depth * rows * (width // chans) * nz * ny
    scale = float(1.0 / count**0.5)
    filter_grad = call(
        functools.partial(final_kernel, chans=chans, scale=scale),
        [jax.ShapeDtypeStruct(filters.shape[::-1], F32)],
        2,
        flag=True,
    )(flag, total, other)
    return (in_grad, filter_grad.T)


def solution(mesh):
    placed = (P("gz", "ch", None), P("gz", "ch", None), P())
    return jax.shard_map(
        per_device,
        mesh=mesh,
        in_specs=placed,
        out_specs=(P("gz", "ch", None), P()),
        check_vma=False,
    )
```

```python
import functools

import jax
import jax.numpy as jnp
from jax import lax
from jax.experimental import pallas as pl
from jax.experimental.pallas import tpu as pltpu
from jax.sharding import PartitionSpec as P

LANES = 128
TAPS = 3
ORDER = (0, 2, 1)
F32 = jnp.float32
BF16 = jnp.bfloat16


def windows(layer):
    width = layer.shape[1]
    moved = pltpu.roll(layer, LANES // 2, axis=1)
    tiles = [moved[:, at : at + LANES] for at in range(0, width, LANES)]
    left = jnp.concatenate(tiles, axis=0)
    right = jnp.concatenate(tiles[1:] + tiles[:1], axis=0)
    return jnp.concatenate([left, right], axis=1).astype(BF16)


def stacked(layer):
    return jnp.concatenate(
        [layer[:, at : at + LANES] for at in range(0, layer.shape[1], LANES)], axis=0
    )


def prep_kernel(og_ref, in_ref, f_ref, e_ref, w_ref, t_ref):
    depth, rows = og_ref.shape[:2]
    chans = f_ref.shape[0]
    cells = LANES // chans
    for z in range(depth):
        e_ref[z] = windows(og_ref[z].astype(F32))
    filters = f_ref[...]
    source = lax.broadcasted_iota(jnp.int32, (chans, 2 * LANES), 0)
    target = lax.broadcasted_iota(jnp.int32, (chans, 2 * LANES), 1)
    placed = {}
    for spot in range(1, cells + 3):
        choose = jnp.where(target == source + spot * chans, 1.0, 0.0).astype(BF16)
        placed[spot] = lax.dot_general(
            filters, choose, (((0,), (0,)), ((), ())), preferred_element_type=F32
        )
    for kz in range(TAPS):
        for slot, ky in enumerate(ORDER):
            for b in range(cells):
                total = None
                for kx in range(TAPS):
                    row = ((kz * TAPS + ky) * TAPS + kx) * chans
                    part = placed[b - kx + 3][row : row + chans]
                    total = part if total is None else total + part
                at = slot * LANES + b * chans
                w_ref[kz, at : at + chans] = total.astype(BF16)
    y = lax.broadcasted_iota(jnp.int32, in_ref.shape[1:], 0)
    for ky in range(TAPS):
        shifted = []
        for z in range(depth):
            layer = in_ref[z].astype(F32)
            if ky != 1:
                layer = jnp.where(y == (0 if ky == 0 else rows - 1), 0.0, pltpu.roll(layer, (1 - ky) % rows, axis=0))
            shifted.append(stacked(layer))
        t_ref[ky * LANES : (ky + 1) * LANES] = jnp.concatenate(shifted, axis=0).astype(BF16).T


def diagonal(product, chans):
    cells = LANES // chans
    lane = lax.broadcasted_iota(jnp.int32, (chans, LANES), 1)
    total = product[(cells - 1) * chans :, LANES:]
    for b in range(cells - 1):
        part = product[b * chans : (b + 1) * chans]
        part = jnp.where(lane >= (b + 1) * chans, part[:, :LANES], part[:, LANES:])
        total = total + pltpu.roll(part, LANES - (b + 1) * chans, axis=1)
    return total


def corners():
    return lax.axis_index("gz") % 2 == 0, lax.axis_index("ch") % 2 == 0


def pack(pairs, chans):
    lane = lax.broadcasted_iota(jnp.int32, (chans, LANES), 1)
    valid = TAPS * chans
    halves = []
    for kz, first in ((2, 0), (0, 5)):
        blocks = []
        for ky in range(TAPS):
            source, place = divmod(first + ky, TAPS)
            extra = pairs[1][source]
            if extra is None:
                extra = jnp.zeros((chans, LANES), F32)
            else:
                extra = pltpu.roll(extra, (valid - place * chans) % LANES, axis=1) if place < TAPS else extra
            main = pairs[kz][ky]
            main = jnp.zeros((chans, LANES), F32) if main is None else main
            blocks.append(jnp.where(lane < valid, main, extra))
        tail = jnp.zeros((chans // 2, LANES), F32)
        for number in range(2):
            piece = first + TAPS + number
            if piece >= min(TAPS * TAPS, first + 5):
                continue
            source, place = divmod(piece, TAPS)
            if pairs[1][source] is None:
                continue
            for part in range(2):
                at = number * 2 + part
                value = pairs[1][source][part * chans // 2 : (part + 1) * chans // 2]
                if at != place:
                    value = pltpu.roll(value, (at - place) * chans % LANES, axis=1)
                tail = jnp.where(lane[: chans // 2] // chans == at, value, tail)
        halves.append(jnp.concatenate(blocks + [tail], axis=0))
    return halves


def own_kernel(t_ref, near_ref, e_ref, og_ref, part_ref, en_ref, r_ref, *, chans):
    core, _ = corners()
    depth, rows, width = og_ref.shape
    near = near_ref[...].astype(F32)
    en = windows(near)
    en_ref[...] = en
    zero = jnp.zeros_like(en)
    own = [e_ref[z] for z in range(depth)]
    every = [jnp.where(core, zero, en)] + own + [jnp.where(core, en, zero)]
    pairs = []
    for kz in range(TAPS):
        window = jnp.concatenate(every[2 - kz : 2 - kz + depth], axis=0)
        product = jnp.dot(t_ref[...], window, preferred_element_type=F32)
        pairs.append([diagonal(product[ky * LANES : (ky + 1) * LANES], chans) for ky in range(TAPS)])
    low, high = pack(pairs, chans)
    part_ref[0] = low
    part_ref[1] = high
    layers = [jnp.where(core, 0.0, near)] + [og_ref[z].astype(F32) for z in range(depth)] + [jnp.where(core, near, 0.0)]
    blank = jnp.zeros((depth + 2, width), F32)
    top = jnp.concatenate([layer[0:1] for layer in layers] + [blank], axis=0)
    end = jnp.concatenate([blank] + [layer[rows - 1 : rows] for layer in layers], axis=0)
    r_ref[:, : 2 * LANES] = windows(top)
    r_ref[:, 2 * LANES :] = windows(end)


def cross_kernel(part_ref, t_ref, r_ref, rowa_ref, rowb_ref, keep_ref, send_ref, vf_ref, *, chans):
    core, even = corners()
    depth, width = rowa_ref.shape
    rows = 2 * (depth + 2)
    rowa, rowb = rowa_ref[...].astype(F32), rowb_ref[...].astype(F32)
    lo, hi = jnp.where(even, rowb, rowa), jnp.where(even, rowa, rowb)
    blank = jnp.zeros((2, width), F32)
    base = jnp.concatenate([blank, lo, blank, hi], axis=0)
    left = [stacked(base if kz == 0 else pltpu.roll(base, rows - kz, axis=0)).astype(BF16) for kz in range(TAPS)]
    left = jnp.concatenate(left, axis=1).T
    product = jnp.dot(left, r_ref[...], preferred_element_type=F32)
    pairs = []
    for kz in range(TAPS):
        both = product[kz * LANES : (kz + 1) * LANES]
        pairs.append([diagonal(both[:, : 2 * LANES], chans), None, diagonal(both[:, 2 * LANES :], chans)])
    low, high = pack(pairs, chans)
    low, high = low + part_ref[0], high + part_ref[1]
    keep_ref[...] = jnp.where(core, low, high)
    send_ref[...] = jnp.where(core, high, low)
    y = lax.broadcasted_iota(jnp.int32, (rows, width), 0)
    edge = jnp.where(
        y == 0, jnp.where(core, lo[0:1], lo[depth - 1 : depth]), jnp.where(core, hi[0:1], hi[depth - 1 : depth])
    )
    edge = stacked(edge).astype(BF16).T
    span = edge.shape[1]
    lane = lax.broadcasted_iota(jnp.int32, edge.shape, 1) % rows
    for ky in range(TAPS):
        block = t_ref[ky * LANES : (ky + 1) * LANES]
        value = jnp.where(core, block[:, :span], block[:, (depth - 1) * span :])
        if ky != 1:
            value = jnp.where(lane == (0 if ky == 0 else rows - 1), edge, value)
        vf_ref[ky * LANES : (ky + 1) * LANES] = value


def far_kernel(vf_ref, far_ref, ef_ref, sum_ref, *, chans):
    window = windows(far_ref[...].astype(F32))
    ef_ref[...] = window
    product = jnp.dot(vf_ref[...], window, preferred_element_type=F32)
    lane = lax.broadcasted_iota(jnp.int32, (chans, LANES), 1)
    for ky in range(TAPS):
        pair = diagonal(product[ky * LANES : (ky + 1) * LANES], chans)
        sum_ref[ky * chans : (ky + 1) * chans] = jnp.where(lane < TAPS * chans, pair, 0.0)
    sum_ref[TAPS * chans :] = jnp.zeros((chans // 2, LANES), F32)


def edge_kernel(og_ref, near_ref, far_ref, first_ref, second_ref):
    core, even = corners()
    depth, rows, _ = og_ref.shape
    near, far = near_ref[...].astype(F32), far_ref[...].astype(F32)
    layers = [jnp.where(core, far, near)] + [og_ref[z].astype(F32) for z in range(depth)] + [jnp.where(core, near, far)]
    tops = jnp.concatenate([layer[0:1] for layer in layers], axis=0)
    ends = jnp.concatenate([layer[rows - 1 : rows] for layer in layers], axis=0)
    first_ref[...] = jnp.where(even, ends, tops).astype(BF16)
    second_ref[...] = jnp.where(even, tops, ends).astype(BF16)


def grad_kernel(e_ref, en_ref, ef_ref, w_ref, rowa_ref, rowb_ref, out_ref):
    depth, rows, width = out_ref.shape
    blocks = width // LANES
    core, even = corners()
    near, far = en_ref[...], ef_ref[...]
    every = [jnp.where(core, far, near)] + [e_ref[z] for z in range(depth)] + [jnp.where(core, near, far)]
    turned = (((1,), (1,)), ((), ()))
    rowa, rowb = rowa_ref[...].astype(F32), rowb_ref[...].astype(F32)
    edges = windows(jnp.concatenate([jnp.where(even, rowb, rowa), jnp.where(even, rowa, rowb)], axis=0))
    layers = depth + 2
    side = None
    for kz in range(TAPS):
        part = lax.dot_general(edges, w_ref[kz, : 2 * LANES], turned, preferred_element_type=F32)
        part = part.reshape(blocks, 2 * layers, 2 * LANES)
        if kz < 2:
            part = pltpu.roll(part, 2 * layers - (2 - kz), axis=1)
        side = part if side is None else side + part
    y = lax.broadcasted_iota(jnp.int32, (blocks, rows, LANES), 1)
    for z in range(depth):
        total = None
        for kz in range(TAPS):
            part = lax.dot_general(every[z - kz + 2], w_ref[kz], turned, preferred_element_type=F32)
            total = part if total is None else total + part
        total = total.reshape(blocks, rows, TAPS * LANES)
        up, down, centre = (total[:, :, slot * LANES : (slot + 1) * LANES] for slot in range(TAPS))
        from_hi = pltpu.roll(side[:, :, :LANES], (rows - 1 - layers - z) % rows, axis=1)
        from_lo = pltpu.roll(side[:, :, LANES:], (rows - z) % rows, axis=1)
        up = jnp.where(y == rows - 1, from_hi, pltpu.roll(up, rows - 1, axis=1))
        down = jnp.where(y == 0, from_lo, pltpu.roll(down, 1, axis=1))
        result = (centre + up + down).astype(BF16)
        for j in range(blocks):
            out_ref[z, :, j * LANES : (j + 1) * LANES] = result[j]


def final_kernel(own_ref, other_ref, out_ref, *, chans, scale):
    core, _ = corners()
    own, other = own_ref[...] * scale, other_ref[...] * scale
    halves = jnp.where(core, own, other), jnp.where(core, other, own)
    for (kz, first), half in zip(((2, 0), (0, 5)), halves):
        turned = half[: TAPS * chans].T
        for ky in range(TAPS):
            block = turned[:, ky * chans : (ky + 1) * chans]
            for kx in range(TAPS):
                place = TAPS - 1 - kx
                at = ((kz * TAPS + ky) * TAPS + kx) * chans
                out_ref[:, at : at + chans] = block[place * chans : (place + 1) * chans]
            source, place = divmod(first + ky, TAPS)
            at = ((TAPS + source) * TAPS + TAPS - 1 - place) * chans
            out_ref[:, at : at + chans] = block[TAPS * chans :]
        tail = half[TAPS * chans :].T
        for number in range(2):
            piece = first + TAPS + number
            if piece >= min(TAPS * TAPS, first + 5):
                continue
            source, place = divmod(piece, TAPS)
            at = ((TAPS + source) * TAPS + TAPS - 1 - place) * chans
            for part in range(2):
                row = (number * 2 + part) * chans
                out_ref[:, at + part * chans // 2 : at + (part + 1) * chans // 2] = tail[row : row + chans]


def call(kernel, outs, n_in, cost=0):
    vmem = pl.BlockSpec(memory_space=pltpu.VMEM)
    single = len(outs) == 1
    return pl.pallas_call(
        kernel,
        out_shape=outs[0] if single else outs,
        in_specs=[vmem] * n_in,
        out_specs=vmem if single else [vmem] * len(outs),
        compiler_params=pltpu.CompilerParams(vmem_limit_bytes=40 * 1024 * 1024),
        cost_estimate=pl.CostEstimate(flops=cost, bytes_accessed=1 << 20, transcendentals=0),
    )


def steps(size):
    rounds, stride = [], 1
    while size > 1:
        factor = next(f for f in range(2, size + 1) if size % f == 0)

        def move(k, stride=stride, factor=factor):
            return lambda p: p + ((p // stride + k) % factor - p // stride % factor) * stride

        rounds.append([move(k) for k in range(1, factor)])
        stride *= factor
        size //= factor
    return rounds


def per_device(inputs, out_grad, filters):
    depth, rows, width = inputs.shape
    chans = filters.shape[1]
    blocks = width // LANES
    nz, ny = lax.axis_size("gz"), lax.axis_size("ch")
    gz, ch = lax.axis_index("gz"), lax.axis_index("ch")

    def over(axis, value, move):
        size = lax.axis_size(axis)
        return lax.ppermute(value, axis, [(p, move(p)) for p in range(size)])

    core, even = gz % 2 == 0, ch % 2 == 0
    here = lambda p: p ^ 1
    there = lambda n: lambda p: (p + (1 if p % 2 else -1)) % n
    layerb = over("gz", jnp.where(core, out_grad[0], out_grad[depth - 1]), there(nz))
    layera = over("gz", jnp.where(core, out_grad[depth - 1], out_grad[0]), here)
    rowb = over("ch", jnp.where(even, inputs[:, 0], inputs[:, rows - 1]), there(ny))
    rowa = over("ch", jnp.where(even, inputs[:, rows - 1], inputs[:, 0]), here)

    wide = jax.ShapeDtypeStruct((blocks * rows, 2 * LANES), BF16)
    e, w, turned = call(
        prep_kernel,
        [
            jax.ShapeDtypeStruct((depth,) + wide.shape, BF16),
            jax.ShapeDtypeStruct((TAPS, TAPS * LANES, 2 * LANES), BF16),
            jax.ShapeDtypeStruct((TAPS * LANES, depth * blocks * rows), BF16),
        ],
        3,
        cost=1 << 29,
    )(out_grad, inputs, filters.T)

    span = blocks * rows
    half = jax.ShapeDtypeStruct((TAPS * chans + chans // 2, LANES), F32)
    edge = jax.ShapeDtypeStruct((depth + 2, width), BF16)
    part, en, r = call(
        functools.partial(own_kernel, chans=chans),
        [
            jax.ShapeDtypeStruct((2,) + half.shape, F32),
            wide,
            jax.ShapeDtypeStruct((span, 4 * LANES), BF16),
        ],
        4,
        cost=1 << 29,
    )(turned, layera, e, out_grad)
    keep, send, vf = call(
        functools.partial(cross_kernel, chans=chans),
        [half, half, jax.ShapeDtypeStruct((TAPS * LANES, span), BF16)],
        5,
        cost=1 << 28,
    )(part, turned, r, rowa, rowb)
    got = over("gz", send, here)
    ef, added = call(functools.partial(far_kernel, chans=chans), [wide, half], 2, cost=1 << 28)(vf, layerb)
    total = keep + got + added
    total, layera, layerb = lax.optimization_barrier((total, layera, layerb))
    first, second = call(edge_kernel, [edge, edge], 3)(out_grad, layera, layerb)

    rounds = [("gz", [lambda p, m=m: m(p // 2) * 2 + p % 2 for m in moves]) for moves in steps(nz // 2)]
    rounds += [("ch", moves) for moves in steps(ny)]
    recva, recvb = over("ch", first, here), over("ch", second, there(ny))
    for number, (axis, moves) in enumerate(rounds):
        got = [over(axis, total, move) for move in moves]
        for value in got:
            total = total + value
        if number == len(rounds) - 1:
            in_grad = call(grad_kernel, [jax.ShapeDtypeStruct(inputs.shape, BF16)], 6, cost=1 << 30)(
                e, en, ef, w, recva, recvb
            )
            total, in_grad = lax.optimization_barrier((total, in_grad))
    other = over("gz", total, here)
    count = depth * rows * (width // chans) * nz * ny
    scale = float(1.0 / count**0.5)
    filter_grad = call(
        functools.partial(final_kernel, chans=chans, scale=scale), [jax.ShapeDtypeStruct(filters.shape[::-1], F32)], 2
    )(total, other)
    return (in_grad, filter_grad.T)


def solution(mesh):
    placed = (P("gz", "ch", None), P("gz", "ch", None), P())
    return jax.shard_map(
        per_device,
        mesh=mesh,
        in_specs=placed,
        out_specs=(P("gz", "ch", None), P()),
        check_vma=False,
    )
```

```python
import functools

import jax
import jax.numpy as jnp
from jax import lax
from jax.experimental import pallas as pl
from jax.experimental.pallas import tpu as pltpu
from jax.sharding import PartitionSpec as P

LANES = 128
TAPS = 3
ORDER = (0, 2, 1)
F32 = jnp.float32
BF16 = jnp.bfloat16


def windows(layer):
    width = layer.shape[1]
    moved = pltpu.roll(layer, LANES // 2, axis=1)
    tiles = [moved[:, at : at + LANES] for at in range(0, width, LANES)]
    left = jnp.concatenate(tiles, axis=0)
    right = jnp.concatenate(tiles[1:] + tiles[:1], axis=0)
    return jnp.concatenate([left, right], axis=1).astype(BF16)


def stacked(layer):
    return jnp.concatenate(
        [layer[:, at : at + LANES] for at in range(0, layer.shape[1], LANES)], axis=0
    )


def prep_kernel(og_ref, in_ref, f_ref, e_ref, w_ref, t_ref):
    depth, rows = og_ref.shape[:2]
    chans = f_ref.shape[0]
    cells = LANES // chans
    for z in range(depth):
        e_ref[z] = windows(og_ref[z].astype(F32))
    filters = f_ref[...]
    source = lax.broadcasted_iota(jnp.int32, (chans, 2 * LANES), 0)
    target = lax.broadcasted_iota(jnp.int32, (chans, 2 * LANES), 1)
    placed = {}
    for spot in range(1, cells + 3):
        choose = jnp.where(target == source + spot * chans, 1.0, 0.0).astype(BF16)
        placed[spot] = lax.dot_general(
            filters, choose, (((0,), (0,)), ((), ())), preferred_element_type=F32
        )
    for kz in range(TAPS):
        for slot, ky in enumerate(ORDER):
            for b in range(cells):
                total = None
                for kx in range(TAPS):
                    row = ((kz * TAPS + ky) * TAPS + kx) * chans
                    part = placed[b - kx + 3][row : row + chans]
                    total = part if total is None else total + part
                at = slot * LANES + b * chans
                w_ref[kz, at : at + chans] = total.astype(BF16)
    y = lax.broadcasted_iota(jnp.int32, in_ref.shape[1:], 0)
    for ky in range(TAPS):
        shifted = []
        for z in range(depth):
            layer = in_ref[z].astype(F32)
            if ky != 1:
                layer = jnp.where(y == (0 if ky == 0 else rows - 1), 0.0, pltpu.roll(layer, (1 - ky) % rows, axis=0))
            shifted.append(stacked(layer))
        t_ref[ky * LANES : (ky + 1) * LANES] = jnp.concatenate(shifted, axis=0).astype(BF16).T


def diagonal(product, chans):
    cells = LANES // chans
    lane = lax.broadcasted_iota(jnp.int32, (chans, LANES), 1)
    total = product[(cells - 1) * chans :, LANES:]
    for b in range(cells - 1):
        part = product[b * chans : (b + 1) * chans]
        part = jnp.where(lane >= (b + 1) * chans, part[:, :LANES], part[:, LANES:])
        total = total + pltpu.roll(part, LANES - (b + 1) * chans, axis=1)
    return total


def corners():
    return lax.axis_index("gz") % 2 == 0, lax.axis_index("ch") % 2 == 0


def pack(pairs, chans):
    lane = lax.broadcasted_iota(jnp.int32, (chans, LANES), 1)
    valid = TAPS * chans
    halves = []
    for kz, first in ((2, 0), (0, 5)):
        blocks = []
        for ky in range(TAPS):
            source, place = divmod(first + ky, TAPS)
            extra = pairs[1][source]
            if extra is None:
                extra = jnp.zeros((chans, LANES), F32)
            else:
                extra = pltpu.roll(extra, (valid - place * chans) % LANES, axis=1) if place < TAPS else extra
            main = pairs[kz][ky]
            main = jnp.zeros((chans, LANES), F32) if main is None else main
            blocks.append(jnp.where(lane < valid, main, extra))
        tail = jnp.zeros((chans // 2, LANES), F32)
        for number in range(2):
            piece = first + TAPS + number
            if piece >= min(TAPS * TAPS, first + 5):
                continue
            source, place = divmod(piece, TAPS)
            if pairs[1][source] is None:
                continue
            for part in range(2):
                at = number * 2 + part
                value = pairs[1][source][part * chans // 2 : (part + 1) * chans // 2]
                if at != place:
                    value = pltpu.roll(value, (at - place) * chans % LANES, axis=1)
                tail = jnp.where(lane[: chans // 2] // chans == at, value, tail)
        halves.append(jnp.concatenate(blocks + [tail], axis=0))
    return halves


def own_kernel(t_ref, near_ref, e_ref, og_ref, part_ref, en_ref, r_ref, *, chans):
    core, _ = corners()
    depth, rows, width = og_ref.shape
    near = near_ref[...].astype(F32)
    en = windows(near)
    en_ref[...] = en
    zero = jnp.zeros_like(en)
    own = [e_ref[z] for z in range(depth)]
    every = [jnp.where(core, zero, en)] + own + [jnp.where(core, en, zero)]
    pairs = []
    for kz in range(TAPS):
        window = jnp.concatenate(every[2 - kz : 2 - kz + depth], axis=0)
        product = jnp.dot(t_ref[...], window, preferred_element_type=F32)
        pairs.append([diagonal(product[ky * LANES : (ky + 1) * LANES], chans) for ky in range(TAPS)])
    low, high = pack(pairs, chans)
    part_ref[0] = low
    part_ref[1] = high
    layers = [jnp.where(core, 0.0, near)] + [og_ref[z].astype(F32) for z in range(depth)] + [jnp.where(core, near, 0.0)]
    blank = jnp.zeros((depth + 2, width), F32)
    top = jnp.concatenate([layer[0:1] for layer in layers] + [blank], axis=0)
    end = jnp.concatenate([blank] + [layer[rows - 1 : rows] for layer in layers], axis=0)
    r_ref[:, : 2 * LANES] = windows(top)
    r_ref[:, 2 * LANES :] = windows(end)


def cross_kernel(part_ref, t_ref, r_ref, rowa_ref, rowb_ref, keep_ref, send_ref, vf_ref, *, chans):
    core, even = corners()
    depth, width = rowa_ref.shape
    rows = 2 * (depth + 2)
    rowa, rowb = rowa_ref[...].astype(F32), rowb_ref[...].astype(F32)
    lo, hi = jnp.where(even, rowb, rowa), jnp.where(even, rowa, rowb)
    blank = jnp.zeros((2, width), F32)
    base = jnp.concatenate([blank, lo, blank, hi], axis=0)
    left = [stacked(base if kz == 0 else pltpu.roll(base, rows - kz, axis=0)).astype(BF16) for kz in range(TAPS)]
    left = jnp.concatenate(left, axis=1).T
    product = jnp.dot(left, r_ref[...], preferred_element_type=F32)
    pairs = []
    for kz in range(TAPS):
        both = product[kz * LANES : (kz + 1) * LANES]
        pairs.append([diagonal(both[:, : 2 * LANES], chans), None, diagonal(both[:, 2 * LANES :], chans)])
    low, high = pack(pairs, chans)
    low, high = low + part_ref[0], high + part_ref[1]
    keep_ref[...] = jnp.where(core, low, high)
    send_ref[...] = jnp.where(core, high, low)
    y = lax.broadcasted_iota(jnp.int32, (rows, width), 0)
    edge = jnp.where(
        y == 0, jnp.where(core, lo[0:1], lo[depth - 1 : depth]), jnp.where(core, hi[0:1], hi[depth - 1 : depth])
    )
    edge = stacked(edge).astype(BF16).T
    span = edge.shape[1]
    lane = lax.broadcasted_iota(jnp.int32, edge.shape, 1) % rows
    for ky in range(TAPS):
        block = t_ref[ky * LANES : (ky + 1) * LANES]
        value = jnp.where(core, block[:, :span], block[:, (depth - 1) * span :])
        if ky != 1:
            value = jnp.where(lane == (0 if ky == 0 else rows - 1), edge, value)
        vf_ref[ky * LANES : (ky + 1) * LANES] = value


def far_kernel(vf_ref, far_ref, ef_ref, sum_ref, *, chans):
    window = windows(far_ref[...].astype(F32))
    ef_ref[...] = window
    product = jnp.dot(vf_ref[...], window, preferred_element_type=F32)
    lane = lax.broadcasted_iota(jnp.int32, (chans, LANES), 1)
    for ky in range(TAPS):
        pair = diagonal(product[ky * LANES : (ky + 1) * LANES], chans)
        sum_ref[ky * chans : (ky + 1) * chans] = jnp.where(lane < TAPS * chans, pair, 0.0)
    sum_ref[TAPS * chans :] = jnp.zeros((chans // 2, LANES), F32)


def edge_kernel(og_ref, near_ref, far_ref, first_ref, second_ref):
    core, even = corners()
    depth, rows, _ = og_ref.shape
    near, far = near_ref[...].astype(F32), far_ref[...].astype(F32)
    layers = [jnp.where(core, far, near)] + [og_ref[z].astype(F32) for z in range(depth)] + [jnp.where(core, near, far)]
    tops = jnp.concatenate([layer[0:1] for layer in layers], axis=0)
    ends = jnp.concatenate([layer[rows - 1 : rows] for layer in layers], axis=0)
    first_ref[...] = jnp.where(even, ends, tops).astype(BF16)
    second_ref[...] = jnp.where(even, tops, ends).astype(BF16)


def grad_kernel(e_ref, en_ref, ef_ref, w_ref, rowa_ref, rowb_ref, out_ref):
    depth, rows, width = out_ref.shape
    blocks = width // LANES
    core, even = corners()
    near, far = en_ref[...], ef_ref[...]
    every = [jnp.where(core, far, near)] + [e_ref[z] for z in range(depth)] + [jnp.where(core, near, far)]
    turned = (((1,), (1,)), ((), ()))
    rowa, rowb = rowa_ref[...].astype(F32), rowb_ref[...].astype(F32)
    edges = windows(jnp.concatenate([jnp.where(even, rowb, rowa), jnp.where(even, rowa, rowb)], axis=0))
    layers = depth + 2
    side = None
    for kz in range(TAPS):
        part = lax.dot_general(edges, w_ref[kz, : 2 * LANES], turned, preferred_element_type=F32)
        part = part.reshape(blocks, 2 * layers, 2 * LANES)
        if kz < 2:
            part = pltpu.roll(part, 2 * layers - (2 - kz), axis=1)
        side = part if side is None else side + part
    y = lax.broadcasted_iota(jnp.int32, (blocks, rows, LANES), 1)
    for z in range(depth):
        total = None
        for kz in range(TAPS):
            part = lax.dot_general(every[z - kz + 2], w_ref[kz], turned, preferred_element_type=F32)
            total = part if total is None else total + part
        total = total.reshape(blocks, rows, TAPS * LANES)
        up, down, centre = (total[:, :, slot * LANES : (slot + 1) * LANES] for slot in range(TAPS))
        from_hi = pltpu.roll(side[:, :, :LANES], (rows - 1 - layers - z) % rows, axis=1)
        from_lo = pltpu.roll(side[:, :, LANES:], (rows - z) % rows, axis=1)
        up = jnp.where(y == rows - 1, from_hi, pltpu.roll(up, rows - 1, axis=1))
        down = jnp.where(y == 0, from_lo, pltpu.roll(down, 1, axis=1))
        result = (centre + up + down).astype(BF16)
        for j in range(blocks):
            out_ref[z, :, j * LANES : (j + 1) * LANES] = result[j]


def final_kernel(own_ref, other_ref, out_ref, *, chans, scale):
    core, _ = corners()
    own, other = own_ref[...] * scale, other_ref[...] * scale
    halves = jnp.where(core, own, other), jnp.where(core, other, own)
    for (kz, first), half in zip(((2, 0), (0, 5)), halves):
        turned = half[: TAPS * chans].T
        for ky in range(TAPS):
            block = turned[:, ky * chans : (ky + 1) * chans]
            for kx in range(TAPS):
                place = TAPS - 1 - kx
                at = ((kz * TAPS + ky) * TAPS + kx) * chans
                out_ref[:, at : at + chans] = block[place * chans : (place + 1) * chans]
            source, place = divmod(first + ky, TAPS)
            at = ((TAPS + source) * TAPS + TAPS - 1 - place) * chans
            out_ref[:, at : at + chans] = block[TAPS * chans :]
        tail = half[TAPS * chans :].T
        for number in range(2):
            piece = first + TAPS + number
            if piece >= min(TAPS * TAPS, first + 5):
                continue
            source, place = divmod(piece, TAPS)
            at = ((TAPS + source) * TAPS + TAPS - 1 - place) * chans
            for part in range(2):
                row = (number * 2 + part) * chans
                out_ref[:, at + part * chans // 2 : at + (part + 1) * chans // 2] = tail[row : row + chans]


def call(kernel, outs, n_in, cost=0):
    vmem = pl.BlockSpec(memory_space=pltpu.VMEM)
    single = len(outs) == 1
    return pl.pallas_call(
        kernel,
        out_shape=outs[0] if single else outs,
        in_specs=[vmem] * n_in,
        out_specs=vmem if single else [vmem] * len(outs),
        compiler_params=pltpu.CompilerParams(vmem_limit_bytes=40 * 1024 * 1024),
        cost_estimate=pl.CostEstimate(flops=cost, bytes_accessed=1 << 20, transcendentals=0),
    )


def steps(size):
    rounds, stride = [], 1
    while size > 1:
        factor = next(f for f in range(2, size + 1) if size % f == 0)

        def move(k, stride=stride, factor=factor):
            return lambda p: p + ((p // stride + k) % factor - p // stride % factor) * stride

        rounds.append([move(k) for k in range(1, factor)])
        stride *= factor
        size //= factor
    return rounds


def per_device(inputs, out_grad, filters):
    depth, rows, width = inputs.shape
    chans = filters.shape[1]
    blocks = width // LANES
    nz, ny = lax.axis_size("gz"), lax.axis_size("ch")
    gz, ch = lax.axis_index("gz"), lax.axis_index("ch")

    def over(axis, value, move):
        size = lax.axis_size(axis)
        return lax.ppermute(value, axis, [(p, move(p)) for p in range(size)])

    core, even = gz % 2 == 0, ch % 2 == 0
    here = lambda p: p ^ 1
    there = lambda n: lambda p: (p + (1 if p % 2 else -1)) % n
    layerb = over("gz", jnp.where(core, out_grad[0], out_grad[depth - 1]), there(nz))
    layera = over("gz", jnp.where(core, out_grad[depth - 1], out_grad[0]), here)
    rowb = over("ch", jnp.where(even, inputs[:, 0], inputs[:, rows - 1]), there(ny))
    rowa = over("ch", jnp.where(even, inputs[:, rows - 1], inputs[:, 0]), here)

    wide = jax.ShapeDtypeStruct((blocks * rows, 2 * LANES), BF16)
    e, w, turned = call(
        prep_kernel,
        [
            jax.ShapeDtypeStruct((depth,) + wide.shape, BF16),
            jax.ShapeDtypeStruct((TAPS, TAPS * LANES, 2 * LANES), BF16),
            jax.ShapeDtypeStruct((TAPS * LANES, depth * blocks * rows), BF16),
        ],
        3,
        cost=1 << 29,
    )(out_grad, inputs, filters.T)

    span = blocks * rows
    half = jax.ShapeDtypeStruct((TAPS * chans + chans // 2, LANES), F32)
    edge = jax.ShapeDtypeStruct((depth + 2, width), BF16)
    part, en, r = call(
        functools.partial(own_kernel, chans=chans),
        [
            jax.ShapeDtypeStruct((2,) + half.shape, F32),
            wide,
            jax.ShapeDtypeStruct((span, 4 * LANES), BF16),
        ],
        4,
        cost=1 << 29,
    )(turned, layera, e, out_grad)
    keep, send, vf = call(
        functools.partial(cross_kernel, chans=chans),
        [half, half, jax.ShapeDtypeStruct((TAPS * LANES, span), BF16)],
        5,
        cost=1 << 28,
    )(part, turned, r, rowa, rowb)
    got = over("gz", send, here)
    ef, added = call(functools.partial(far_kernel, chans=chans), [wide, half], 2, cost=1 << 28)(vf, layerb)
    total = keep + got + added
    total, layera, layerb = lax.optimization_barrier((total, layera, layerb))
    first, second = call(edge_kernel, [edge, edge], 3)(out_grad, layera, layerb)

    rounds = [("gz", [lambda p, m=m: m(p // 2) * 2 + p % 2 for m in moves]) for moves in steps(nz // 2)]
    rounds += [("ch", moves) for moves in steps(ny)]
    recvb = over("ch", second, there(ny))
    first, recvb = lax.optimization_barrier((first, recvb))
    recva = over("ch", first, here)
    for number, (axis, moves) in enumerate(rounds):
        got = [over(axis, total, move) for move in moves]
        for value in got:
            total = total + value
        if number == len(rounds) - 1:
            in_grad = call(grad_kernel, [jax.ShapeDtypeStruct(inputs.shape, BF16)], 6, cost=1 << 30)(
                e, en, ef, w, recva, recvb
            )
            total, in_grad = lax.optimization_barrier((total, in_grad))
    other = over("gz", total, here)
    count = depth * rows * (width // chans) * nz * ny
    scale = float(1.0 / count**0.5)
    filter_grad = call(
        functools.partial(final_kernel, chans=chans, scale=scale), [jax.ShapeDtypeStruct(filters.shape[::-1], F32)], 2
    )(total, other)
    return (in_grad, filter_grad.T)


def solution(mesh):
    placed = (P("gz", "ch", None), P("gz", "ch", None), P())
    return jax.shard_map(
        per_device,
        mesh=mesh,
        in_specs=placed,
        out_specs=(P("gz", "ch", None), P()),
        check_vma=False,
    )
```

```python
import functools

import jax
import jax.numpy as jnp
from jax import lax
from jax.experimental import pallas as pl
from jax.experimental.pallas import tpu as pltpu
from jax.sharding import PartitionSpec as P

LANES = 128
TAPS = 3
ORDER = (0, 2, 1)
F32 = jnp.float32
BF16 = jnp.bfloat16


def windows(layer):
    width = layer.shape[1]
    moved = pltpu.roll(layer, LANES // 2, axis=1)
    tiles = [moved[:, at : at + LANES] for at in range(0, width, LANES)]
    left = jnp.concatenate(tiles, axis=0)
    right = jnp.concatenate(tiles[1:] + tiles[:1], axis=0)
    return jnp.concatenate([left, right], axis=1).astype(BF16)


def stacked(layer):
    return jnp.concatenate(
        [layer[:, at : at + LANES] for at in range(0, layer.shape[1], LANES)], axis=0
    )


def prep_kernel(og_ref, in_ref, f_ref, e_ref, w_ref, t_ref):
    depth, rows = og_ref.shape[:2]
    chans = f_ref.shape[0]
    cells = LANES // chans
    for z in range(depth):
        e_ref[z] = windows(og_ref[z].astype(F32))
    filters = f_ref[...]
    source = lax.broadcasted_iota(jnp.int32, (chans, 2 * LANES), 0)
    target = lax.broadcasted_iota(jnp.int32, (chans, 2 * LANES), 1)
    placed = {}
    for spot in range(1, cells + 3):
        choose = jnp.where(target == source + spot * chans, 1.0, 0.0).astype(BF16)
        placed[spot] = lax.dot_general(
            filters, choose, (((0,), (0,)), ((), ())), preferred_element_type=F32
        )
    for kz in range(TAPS):
        for slot, ky in enumerate(ORDER):
            for b in range(cells):
                total = None
                for kx in range(TAPS):
                    row = ((kz * TAPS + ky) * TAPS + kx) * chans
                    part = placed[b - kx + 3][row : row + chans]
                    total = part if total is None else total + part
                at = slot * LANES + b * chans
                w_ref[kz, at : at + chans] = total.astype(BF16)
    y = lax.broadcasted_iota(jnp.int32, in_ref.shape[1:], 0)
    for ky in range(TAPS):
        shifted = []
        for z in range(depth):
            layer = in_ref[z].astype(F32)
            if ky != 1:
                layer = jnp.where(y == (0 if ky == 0 else rows - 1), 0.0, pltpu.roll(layer, (1 - ky) % rows, axis=0))
            shifted.append(stacked(layer))
        t_ref[ky * LANES : (ky + 1) * LANES] = jnp.concatenate(shifted, axis=0).astype(BF16).T


def diagonal(product, chans):
    cells = LANES // chans
    lane = lax.broadcasted_iota(jnp.int32, (chans, LANES), 1)
    total = product[(cells - 1) * chans :, LANES:]
    for b in range(cells - 1):
        part = product[b * chans : (b + 1) * chans]
        part = jnp.where(lane >= (b + 1) * chans, part[:, :LANES], part[:, LANES:])
        total = total + pltpu.roll(part, LANES - (b + 1) * chans, axis=1)
    return total


def corners():
    return lax.axis_index("gz") % 2 == 0, lax.axis_index("ch") % 2 == 0


def pack(pairs, chans):
    lane = lax.broadcasted_iota(jnp.int32, (chans, LANES), 1)
    valid = TAPS * chans
    halves = []
    for kz, first in ((2, 0), (0, 5)):
        blocks = []
        for ky in range(TAPS):
            source, place = divmod(first + ky, TAPS)
            extra = pairs[1][source]
            if extra is None:
                extra = jnp.zeros((chans, LANES), F32)
            else:
                extra = pltpu.roll(extra, (valid - place * chans) % LANES, axis=1) if place < TAPS else extra
            main = pairs[kz][ky]
            main = jnp.zeros((chans, LANES), F32) if main is None else main
            blocks.append(jnp.where(lane < valid, main, extra))
        tail = jnp.zeros((chans // 2, LANES), F32)
        for number in range(2):
            piece = first + TAPS + number
            if piece >= min(TAPS * TAPS, first + 5):
                continue
            source, place = divmod(piece, TAPS)
            if pairs[1][source] is None:
                continue
            for part in range(2):
                at = number * 2 + part
                value = pairs[1][source][part * chans // 2 : (part + 1) * chans // 2]
                if at != place:
                    value = pltpu.roll(value, (at - place) * chans % LANES, axis=1)
                tail = jnp.where(lane[: chans // 2] // chans == at, value, tail)
        halves.append(jnp.concatenate(blocks + [tail], axis=0))
    return halves


def own_kernel(t_ref, near_ref, e_ref, og_ref, part_ref, en_ref, r_ref, *, chans):
    core, _ = corners()
    depth, rows, width = og_ref.shape
    near = near_ref[...].astype(F32)
    en = windows(near)
    en_ref[...] = en
    zero = jnp.zeros_like(en)
    own = [e_ref[z] for z in range(depth)]
    every = [jnp.where(core, zero, en)] + own + [jnp.where(core, en, zero)]
    pairs = []
    for kz in range(TAPS):
        window = jnp.concatenate(every[2 - kz : 2 - kz + depth], axis=0)
        product = jnp.dot(t_ref[...], window, preferred_element_type=F32)
        pairs.append([diagonal(product[ky * LANES : (ky + 1) * LANES], chans) for ky in range(TAPS)])
    low, high = pack(pairs, chans)
    part_ref[0] = low
    part_ref[1] = high
    layers = [jnp.where(core, 0.0, near)] + [og_ref[z].astype(F32) for z in range(depth)] + [jnp.where(core, near, 0.0)]
    blank = jnp.zeros((depth + 2, width), F32)
    top = jnp.concatenate([layer[0:1] for layer in layers] + [blank], axis=0)
    end = jnp.concatenate([blank] + [layer[rows - 1 : rows] for layer in layers], axis=0)
    r_ref[:, : 2 * LANES] = windows(top)
    r_ref[:, 2 * LANES :] = windows(end)


def cross_kernel(part_ref, t_ref, r_ref, rowa_ref, rowb_ref, keep_ref, send_ref, vf_ref, *, chans):
    core, even = corners()
    depth, width = rowa_ref.shape
    rows = 2 * (depth + 2)
    rowa, rowb = rowa_ref[...].astype(F32), rowb_ref[...].astype(F32)
    lo, hi = jnp.where(even, rowb, rowa), jnp.where(even, rowa, rowb)
    blank = jnp.zeros((2, width), F32)
    base = jnp.concatenate([blank, lo, blank, hi], axis=0)
    left = [stacked(base if kz == 0 else pltpu.roll(base, rows - kz, axis=0)).astype(BF16) for kz in range(TAPS)]
    left = jnp.concatenate(left, axis=1).T
    product = jnp.dot(left, r_ref[...], preferred_element_type=F32)
    pairs = []
    for kz in range(TAPS):
        both = product[kz * LANES : (kz + 1) * LANES]
        pairs.append([diagonal(both[:, : 2 * LANES], chans), None, diagonal(both[:, 2 * LANES :], chans)])
    low, high = pack(pairs, chans)
    low, high = low + part_ref[0], high + part_ref[1]
    keep_ref[...] = jnp.where(core, low, high)
    send_ref[...] = jnp.where(core, high, low)
    y = lax.broadcasted_iota(jnp.int32, (rows, width), 0)
    edge = jnp.where(
        y == 0, jnp.where(core, lo[0:1], lo[depth - 1 : depth]), jnp.where(core, hi[0:1], hi[depth - 1 : depth])
    )
    edge = stacked(edge).astype(BF16).T
    span = edge.shape[1]
    lane = lax.broadcasted_iota(jnp.int32, edge.shape, 1) % rows
    for ky in range(TAPS):
        block = t_ref[ky * LANES : (ky + 1) * LANES]
        value = jnp.where(core, block[:, :span], block[:, (depth - 1) * span :])
        if ky != 1:
            value = jnp.where(lane == (0 if ky == 0 else rows - 1), edge, value)
        vf_ref[ky * LANES : (ky + 1) * LANES] = value


def far_kernel(vf_ref, far_ref, ef_ref, sum_ref, *, chans):
    window = windows(far_ref[...].astype(F32))
    ef_ref[...] = window
    product = jnp.dot(vf_ref[...], window, preferred_element_type=F32)
    lane = lax.broadcasted_iota(jnp.int32, (chans, LANES), 1)
    for ky in range(TAPS):
        pair = diagonal(product[ky * LANES : (ky + 1) * LANES], chans)
        sum_ref[ky * chans : (ky + 1) * chans] = jnp.where(lane < TAPS * chans, pair, 0.0)
    sum_ref[TAPS * chans :] = jnp.zeros((chans // 2, LANES), F32)


def edge_kernel(og_ref, near_ref, far_ref, first_ref, second_ref):
    core, even = corners()
    depth, rows, _ = og_ref.shape
    near, far = near_ref[...].astype(F32), far_ref[...].astype(F32)
    layers = [jnp.where(core, far, near)] + [og_ref[z].astype(F32) for z in range(depth)] + [jnp.where(core, near, far)]
    tops = jnp.concatenate([layer[0:1] for layer in layers], axis=0)
    ends = jnp.concatenate([layer[rows - 1 : rows] for layer in layers], axis=0)
    first_ref[...] = jnp.where(even, ends, tops).astype(BF16)
    second_ref[...] = jnp.where(even, tops, ends).astype(BF16)


def grad_kernel(e_ref, en_ref, ef_ref, w_ref, rowa_ref, rowb_ref, out_ref):
    depth, rows, width = out_ref.shape
    blocks = width // LANES
    core, even = corners()
    near, far = en_ref[...], ef_ref[...]
    every = [jnp.where(core, far, near)] + [e_ref[z] for z in range(depth)] + [jnp.where(core, near, far)]
    turned = (((1,), (1,)), ((), ()))
    rowa, rowb = rowa_ref[...].astype(F32), rowb_ref[...].astype(F32)
    edges = windows(jnp.concatenate([jnp.where(even, rowb, rowa), jnp.where(even, rowa, rowb)], axis=0))
    layers = depth + 2
    side = None
    for kz in range(TAPS):
        part = lax.dot_general(edges, w_ref[kz, : 2 * LANES], turned, preferred_element_type=F32)
        part = part.reshape(blocks, 2 * layers, 2 * LANES)
        if kz < 2:
            part = pltpu.roll(part, 2 * layers - (2 - kz), axis=1)
        side = part if side is None else side + part
    y = lax.broadcasted_iota(jnp.int32, (blocks, rows, LANES), 1)
    for z in range(depth):
        total = None
        for kz in range(TAPS):
            part = lax.dot_general(every[z - kz + 2], w_ref[kz], turned, preferred_element_type=F32)
            total = part if total is None else total + part
        total = total.reshape(blocks, rows, TAPS * LANES)
        up, down, centre = (total[:, :, slot * LANES : (slot + 1) * LANES] for slot in range(TAPS))
        from_hi = pltpu.roll(side[:, :, :LANES], (rows - 1 - layers - z) % rows, axis=1)
        from_lo = pltpu.roll(side[:, :, LANES:], (rows - z) % rows, axis=1)
        up = jnp.where(y == rows - 1, from_hi, pltpu.roll(up, rows - 1, axis=1))
        down = jnp.where(y == 0, from_lo, pltpu.roll(down, 1, axis=1))
        result = (centre + up + down).astype(BF16)
        for j in range(blocks):
            out_ref[z, :, j * LANES : (j + 1) * LANES] = result[j]


def final_kernel(own_ref, other_ref, out_ref, *, chans, scale):
    core, _ = corners()
    own, other = own_ref[...] * scale, other_ref[...] * scale
    halves = jnp.where(core, own, other), jnp.where(core, other, own)
    for (kz, first), half in zip(((2, 0), (0, 5)), halves):
        turned = half[: TAPS * chans].T
        for ky in range(TAPS):
            block = turned[:, ky * chans : (ky + 1) * chans]
            for kx in range(TAPS):
                place = TAPS - 1 - kx
                at = ((kz * TAPS + ky) * TAPS + kx) * chans
                out_ref[:, at : at + chans] = block[place * chans : (place + 1) * chans]
            source, place = divmod(first + ky, TAPS)
            at = ((TAPS + source) * TAPS + TAPS - 1 - place) * chans
            out_ref[:, at : at + chans] = block[TAPS * chans :]
        tail = half[TAPS * chans :].T
        for number in range(2):
            piece = first + TAPS + number
            if piece >= min(TAPS * TAPS, first + 5):
                continue
            source, place = divmod(piece, TAPS)
            at = ((TAPS + source) * TAPS + TAPS - 1 - place) * chans
            for part in range(2):
                row = (number * 2 + part) * chans
                out_ref[:, at + part * chans // 2 : at + (part + 1) * chans // 2] = tail[row : row + chans]


def call(kernel, outs, n_in, cost=0):
    vmem = pl.BlockSpec(memory_space=pltpu.VMEM)
    single = len(outs) == 1
    return pl.pallas_call(
        kernel,
        out_shape=outs[0] if single else outs,
        in_specs=[vmem] * n_in,
        out_specs=vmem if single else [vmem] * len(outs),
        compiler_params=pltpu.CompilerParams(vmem_limit_bytes=40 * 1024 * 1024),
        cost_estimate=pl.CostEstimate(flops=cost, bytes_accessed=1 << 20, transcendentals=0),
    )


def steps(size):
    stride, found = 1, []
    while size > 1:
        factor = next(f for f in range(2, size + 1) if size % f == 0)
        found.append((stride, factor))
        stride *= factor
        size //= factor
    return found


def shifted(place, dims, step):
    for stride, factor in dims:
        digit = place // stride % factor
        place += ((digit + step % factor) % factor - digit) * stride
        step //= factor
    return place


def per_device(inputs, out_grad, filters):
    depth, rows, width = inputs.shape
    chans = filters.shape[1]
    blocks = width // LANES
    nz, ny = lax.axis_size("gz"), lax.axis_size("ch")
    gz, ch = lax.axis_index("gz"), lax.axis_index("ch")

    def over(axis, value, move):
        size = lax.axis_size(axis)
        return lax.ppermute(value, axis, [(p, move(p)) for p in range(size)])

    core, even = gz % 2 == 0, ch % 2 == 0
    here = lambda p: p ^ 1
    there = lambda n: lambda p: (p + (1 if p % 2 else -1)) % n
    layerb = over("gz", jnp.where(core, out_grad[0], out_grad[depth - 1]), there(nz))
    layera = over("gz", jnp.where(core, out_grad[depth - 1], out_grad[0]), here)
    rowb = over("ch", jnp.where(even, inputs[:, 0], inputs[:, rows - 1]), there(ny))
    rowa = over("ch", jnp.where(even, inputs[:, rows - 1], inputs[:, 0]), here)

    wide = jax.ShapeDtypeStruct((blocks * rows, 2 * LANES), BF16)
    e, w, turned = call(
        prep_kernel,
        [
            jax.ShapeDtypeStruct((depth,) + wide.shape, BF16),
            jax.ShapeDtypeStruct((TAPS, TAPS * LANES, 2 * LANES), BF16),
            jax.ShapeDtypeStruct((TAPS * LANES, depth * blocks * rows), BF16),
        ],
        3,
        cost=1 << 29,
    )(out_grad, inputs, filters.T)

    span = blocks * rows
    half = jax.ShapeDtypeStruct((TAPS * chans + chans // 2, LANES), F32)
    edge = jax.ShapeDtypeStruct((depth + 2, width), BF16)
    part, en, r = call(
        functools.partial(own_kernel, chans=chans),
        [
            jax.ShapeDtypeStruct((2,) + half.shape, F32),
            wide,
            jax.ShapeDtypeStruct((span, 4 * LANES), BF16),
        ],
        4,
        cost=1 << 29,
    )(turned, layera, e, out_grad)
    keep, send, vf = call(
        functools.partial(cross_kernel, chans=chans),
        [half, half, jax.ShapeDtypeStruct((TAPS * LANES, span), BF16)],
        5,
        cost=1 << 28,
    )(part, turned, r, rowa, rowb)
    got = over("gz", send, here)
    ef, added = call(functools.partial(far_kernel, chans=chans), [wide, half], 2, cost=1 << 28)(vf, layerb)
    total = keep + got + added
    total, layera, layerb = lax.optimization_barrier((total, layera, layerb))
    first, second = call(edge_kernel, [edge, edge], 3)(out_grad, layera, layerb)

    plane = [(2 * stride, factor) for stride, factor in steps(nz // 2)]
    rounds = [("gz", plane)] if nz == 8 else [("gz", [dim]) for dim in plane]
    rounds += [("ch", [dim]) for dim in steps(ny)]
    recvb = over("ch", second, there(ny))
    first, recvb = lax.optimization_barrier((first, recvb))
    recva = over("ch", first, here)
    for number, (axis, dims) in enumerate(rounds):
        count = 1
        for _, factor in dims:
            count *= factor
        values = [total]
        for step in range(1, count):
            values.append(over(axis, total, lambda p: shifted(p, dims, step)))
        for stride, factor in dims:
            groups = [values[k : k + factor] for k in range(0, len(values), factor)]
            if factor > 2:
                digit = lax.axis_index(axis) // stride % factor
                groups = [list(jnp.roll(jnp.stack(group), digit, axis=0)) for group in groups]
            values = [functools.reduce(lambda x, y: x + y, group) for group in groups]
        total = values[0]
        if number == len(rounds) - 1:
            in_grad = call(grad_kernel, [jax.ShapeDtypeStruct(inputs.shape, BF16)], 6, cost=1 << 30)(
                e, en, ef, w, recva, recvb
            )
            total, in_grad = lax.optimization_barrier((total, in_grad))
    other = over("gz", total, here)
    count = depth * rows * (width // chans) * nz * ny
    scale = float(1.0 / count**0.5)
    filter_grad = call(
        functools.partial(final_kernel, chans=chans, scale=scale), [jax.ShapeDtypeStruct(filters.shape[::-1], F32)], 2
    )(total, other)
    return (in_grad, filter_grad.T)


def solution(mesh):
    placed = (P("gz", "ch", None), P("gz", "ch", None), P())
    return jax.shard_map(
        per_device,
        mesh=mesh,
        in_specs=placed,
        out_specs=(P("gz", "ch", None), P()),
        check_vma=False,
    )
```

```python
import functools

import jax
import jax.numpy as jnp
from jax import lax
from jax.experimental import pallas as pl
from jax.experimental.pallas import tpu as pltpu
from jax.sharding import PartitionSpec as P

LANES = 128
TAPS = 3
ORDER = (0, 2, 1)
F32 = jnp.float32
BF16 = jnp.bfloat16


def windows(layer):
    width = layer.shape[1]
    moved = pltpu.roll(layer, LANES // 2, axis=1)
    tiles = [moved[:, at : at + LANES] for at in range(0, width, LANES)]
    left = jnp.concatenate(tiles, axis=0)
    right = jnp.concatenate(tiles[1:] + tiles[:1], axis=0)
    return jnp.concatenate([left, right], axis=1).astype(BF16)


def stacked(layer):
    return jnp.concatenate(
        [layer[:, at : at + LANES] for at in range(0, layer.shape[1], LANES)], axis=0
    )


def prep_kernel(og_ref, in_ref, f_ref, e_ref, w_ref, t_ref):
    depth, rows = og_ref.shape[:2]
    chans = f_ref.shape[0]
    cells = LANES // chans
    for z in range(depth):
        e_ref[z] = windows(og_ref[z].astype(F32))
    filters = f_ref[...]
    source = lax.broadcasted_iota(jnp.int32, (chans, 2 * LANES), 0)
    target = lax.broadcasted_iota(jnp.int32, (chans, 2 * LANES), 1)
    placed = {}
    for spot in range(1, cells + 3):
        choose = jnp.where(target == source + spot * chans, 1.0, 0.0).astype(BF16)
        placed[spot] = lax.dot_general(
            filters, choose, (((0,), (0,)), ((), ())), preferred_element_type=F32
        )
    for kz in range(TAPS):
        for slot, ky in enumerate(ORDER):
            for b in range(cells):
                total = None
                for kx in range(TAPS):
                    row = ((kz * TAPS + ky) * TAPS + kx) * chans
                    part = placed[b - kx + 3][row : row + chans]
                    total = part if total is None else total + part
                at = slot * LANES + b * chans
                w_ref[kz, at : at + chans] = total.astype(BF16)
    y = lax.broadcasted_iota(jnp.int32, in_ref.shape[1:], 0)
    for ky in range(TAPS):
        shifted = []
        for z in range(depth):
            layer = in_ref[z].astype(F32)
            if ky != 1:
                layer = jnp.where(y == (0 if ky == 0 else rows - 1), 0.0, pltpu.roll(layer, (1 - ky) % rows, axis=0))
            shifted.append(stacked(layer))
        t_ref[ky * LANES : (ky + 1) * LANES] = jnp.concatenate(shifted, axis=0).astype(BF16).T


def diagonal(product, chans):
    cells = LANES // chans
    lane = lax.broadcasted_iota(jnp.int32, (chans, LANES), 1)
    total = product[(cells - 1) * chans :, LANES:]
    for b in range(cells - 1):
        part = product[b * chans : (b + 1) * chans]
        part = jnp.where(lane >= (b + 1) * chans, part[:, :LANES], part[:, LANES:])
        total = total + pltpu.roll(part, LANES - (b + 1) * chans, axis=1)
    return total


def corners():
    return lax.axis_index("gz") % 2 == 0, lax.axis_index("ch") % 2 == 0


def pack(pairs, chans):
    lane = lax.broadcasted_iota(jnp.int32, (chans, LANES), 1)
    valid = TAPS * chans
    halves = []
    for kz, first in ((2, 0), (0, 5)):
        blocks = []
        for ky in range(TAPS):
            source, place = divmod(first + ky, TAPS)
            extra = pairs[1][source]
            if extra is None:
                extra = jnp.zeros((chans, LANES), F32)
            else:
                extra = pltpu.roll(extra, (valid - place * chans) % LANES, axis=1) if place < TAPS else extra
            main = pairs[kz][ky]
            main = jnp.zeros((chans, LANES), F32) if main is None else main
            blocks.append(jnp.where(lane < valid, main, extra))
        tail = jnp.zeros((chans // 2, LANES), F32)
        for number in range(2):
            piece = first + TAPS + number
            if piece >= min(TAPS * TAPS, first + 5):
                continue
            source, place = divmod(piece, TAPS)
            if pairs[1][source] is None:
                continue
            for part in range(2):
                at = number * 2 + part
                value = pairs[1][source][part * chans // 2 : (part + 1) * chans // 2]
                if at != place:
                    value = pltpu.roll(value, (at - place) * chans % LANES, axis=1)
                tail = jnp.where(lane[: chans // 2] // chans == at, value, tail)
        halves.append(jnp.concatenate(blocks + [tail], axis=0))
    return halves


def own_kernel(t_ref, near_ref, e_ref, og_ref, part_ref, en_ref, r_ref, *, chans):
    core, _ = corners()
    depth, rows, width = og_ref.shape
    near = near_ref[...].astype(F32)
    en = windows(near)
    en_ref[...] = en
    zero = jnp.zeros_like(en)
    own = [e_ref[z] for z in range(depth)]
    every = [jnp.where(core, zero, en)] + own + [jnp.where(core, en, zero)]
    pairs = []
    for kz in range(TAPS):
        window = jnp.concatenate(every[2 - kz : 2 - kz + depth], axis=0)
        product = jnp.dot(t_ref[...], window, preferred_element_type=F32)
        pairs.append([diagonal(product[ky * LANES : (ky + 1) * LANES], chans) for ky in range(TAPS)])
    low, high = pack(pairs, chans)
    part_ref[0] = low
    part_ref[1] = high
    layers = [jnp.where(core, 0.0, near)] + [og_ref[z].astype(F32) for z in range(depth)] + [jnp.where(core, near, 0.0)]
    blank = jnp.zeros((depth + 2, width), F32)
    top = jnp.concatenate([layer[0:1] for layer in layers] + [blank], axis=0)
    end = jnp.concatenate([blank] + [layer[rows - 1 : rows] for layer in layers], axis=0)
    r_ref[:, : 2 * LANES] = windows(top)
    r_ref[:, 2 * LANES :] = windows(end)


def cross_kernel(part_ref, t_ref, r_ref, rowa_ref, rowb_ref, keep_ref, send_ref, vf_ref, *, chans):
    core, even = corners()
    depth, width = rowa_ref.shape
    rows = 2 * (depth + 2)
    rowa, rowb = rowa_ref[...].astype(F32), rowb_ref[...].astype(F32)
    lo, hi = jnp.where(even, rowb, rowa), jnp.where(even, rowa, rowb)
    blank = jnp.zeros((2, width), F32)
    base = jnp.concatenate([blank, lo, blank, hi], axis=0)
    left = [stacked(base if kz == 0 else pltpu.roll(base, rows - kz, axis=0)).astype(BF16) for kz in range(TAPS)]
    left = jnp.concatenate(left, axis=1).T
    product = jnp.dot(left, r_ref[...], preferred_element_type=F32)
    pairs = []
    for kz in range(TAPS):
        both = product[kz * LANES : (kz + 1) * LANES]
        pairs.append([diagonal(both[:, : 2 * LANES], chans), None, diagonal(both[:, 2 * LANES :], chans)])
    low, high = pack(pairs, chans)
    low, high = low + part_ref[0], high + part_ref[1]
    keep_ref[...] = jnp.where(core, low, high)
    send_ref[...] = jnp.where(core, high, low)
    y = lax.broadcasted_iota(jnp.int32, (rows, width), 0)
    edge = jnp.where(
        y == 0, jnp.where(core, lo[0:1], lo[depth - 1 : depth]), jnp.where(core, hi[0:1], hi[depth - 1 : depth])
    )
    edge = stacked(edge).astype(BF16).T
    span = edge.shape[1]
    lane = lax.broadcasted_iota(jnp.int32, edge.shape, 1) % rows
    for ky in range(TAPS):
        block = t_ref[ky * LANES : (ky + 1) * LANES]
        value = jnp.where(core, block[:, :span], block[:, (depth - 1) * span :])
        if ky != 1:
            value = jnp.where(lane == (0 if ky == 0 else rows - 1), edge, value)
        vf_ref[ky * LANES : (ky + 1) * LANES] = value


def far_kernel(vf_ref, far_ref, ef_ref, sum_ref, *, chans):
    window = windows(far_ref[...].astype(F32))
    ef_ref[...] = window
    product = jnp.dot(vf_ref[...], window, preferred_element_type=F32)
    lane = lax.broadcasted_iota(jnp.int32, (chans, LANES), 1)
    for ky in range(TAPS):
        pair = diagonal(product[ky * LANES : (ky + 1) * LANES], chans)
        sum_ref[ky * chans : (ky + 1) * chans] = jnp.where(lane < TAPS * chans, pair, 0.0)
    sum_ref[TAPS * chans :] = jnp.zeros((chans // 2, LANES), F32)


def edge_kernel(og_ref, near_ref, far_ref, first_ref, second_ref):
    core, even = corners()
    depth, rows, _ = og_ref.shape
    near, far = near_ref[...].astype(F32), far_ref[...].astype(F32)
    layers = [jnp.where(core, far, near)] + [og_ref[z].astype(F32) for z in range(depth)] + [jnp.where(core, near, far)]
    tops = jnp.concatenate([layer[0:1] for layer in layers], axis=0)
    ends = jnp.concatenate([layer[rows - 1 : rows] for layer in layers], axis=0)
    first_ref[...] = jnp.where(even, ends, tops).astype(BF16)
    second_ref[...] = jnp.where(even, tops, ends).astype(BF16)


def grad_kernel(e_ref, en_ref, ef_ref, w_ref, rowa_ref, rowb_ref, out_ref):
    depth, rows, width = out_ref.shape
    blocks = width // LANES
    core, even = corners()
    near, far = en_ref[...], ef_ref[...]
    every = [jnp.where(core, far, near)] + [e_ref[z] for z in range(depth)] + [jnp.where(core, near, far)]
    turned = (((1,), (1,)), ((), ()))
    rowa, rowb = rowa_ref[...].astype(F32), rowb_ref[...].astype(F32)
    edges = windows(jnp.concatenate([jnp.where(even, rowb, rowa), jnp.where(even, rowa, rowb)], axis=0))
    layers = depth + 2
    side = None
    for kz in range(TAPS):
        part = lax.dot_general(edges, w_ref[kz, : 2 * LANES], turned, preferred_element_type=F32)
        part = part.reshape(blocks, 2 * layers, 2 * LANES)
        if kz < 2:
            part = pltpu.roll(part, 2 * layers - (2 - kz), axis=1)
        side = part if side is None else side + part
    y = lax.broadcasted_iota(jnp.int32, (blocks, rows, LANES), 1)
    for z in range(depth):
        total = None
        for kz in range(TAPS):
            part = lax.dot_general(every[z - kz + 2], w_ref[kz], turned, preferred_element_type=F32)
            total = part if total is None else total + part
        total = total.reshape(blocks, rows, TAPS * LANES)
        up, down, centre = (total[:, :, slot * LANES : (slot + 1) * LANES] for slot in range(TAPS))
        from_hi = pltpu.roll(side[:, :, :LANES], (rows - 1 - layers - z) % rows, axis=1)
        from_lo = pltpu.roll(side[:, :, LANES:], (rows - z) % rows, axis=1)
        up = jnp.where(y == rows - 1, from_hi, pltpu.roll(up, rows - 1, axis=1))
        down = jnp.where(y == 0, from_lo, pltpu.roll(down, 1, axis=1))
        result = (centre + up + down).astype(BF16)
        for j in range(blocks):
            out_ref[z, :, j * LANES : (j + 1) * LANES] = result[j]


def final_kernel(own_ref, other_ref, out_ref, *, chans, scale):
    core, _ = corners()
    own, other = own_ref[...] * scale, other_ref[...] * scale
    halves = jnp.where(core, own, other), jnp.where(core, other, own)
    for (kz, first), half in zip(((2, 0), (0, 5)), halves):
        turned = half[: TAPS * chans].T
        for ky in range(TAPS):
            block = turned[:, ky * chans : (ky + 1) * chans]
            for kx in range(TAPS):
                place = TAPS - 1 - kx
                at = ((kz * TAPS + ky) * TAPS + kx) * chans
                out_ref[:, at : at + chans] = block[place * chans : (place + 1) * chans]
            source, place = divmod(first + ky, TAPS)
            at = ((TAPS + source) * TAPS + TAPS - 1 - place) * chans
            out_ref[:, at : at + chans] = block[TAPS * chans :]
        tail = half[TAPS * chans :].T
        for number in range(2):
            piece = first + TAPS + number
            if piece >= min(TAPS * TAPS, first + 5):
                continue
            source, place = divmod(piece, TAPS)
            at = ((TAPS + source) * TAPS + TAPS - 1 - place) * chans
            for part in range(2):
                row = (number * 2 + part) * chans
                out_ref[:, at + part * chans // 2 : at + (part + 1) * chans // 2] = tail[row : row + chans]


def call(kernel, outs, n_in, cost=0):
    vmem = pl.BlockSpec(memory_space=pltpu.VMEM)
    single = len(outs) == 1
    return pl.pallas_call(
        kernel,
        out_shape=outs[0] if single else outs,
        in_specs=[vmem] * n_in,
        out_specs=vmem if single else [vmem] * len(outs),
        compiler_params=pltpu.CompilerParams(vmem_limit_bytes=40 * 1024 * 1024),
        cost_estimate=pl.CostEstimate(flops=cost, bytes_accessed=1 << 20, transcendentals=0),
    )


def steps(size):
    stride, found = 1, []
    while size > 1:
        factor = next(f for f in range(2, size + 1) if size % f == 0)
        found.append((stride, factor))
        stride *= factor
        size //= factor
    return found


def shifted(place, dims, step):
    for stride, factor in dims:
        digit = place // stride % factor
        place += ((digit + step % factor) % factor - digit) * stride
        step //= factor
    return place


def per_device(inputs, out_grad, filters):
    depth, rows, width = inputs.shape
    chans = filters.shape[1]
    blocks = width // LANES
    nz, ny = lax.axis_size("gz"), lax.axis_size("ch")
    gz, ch = lax.axis_index("gz"), lax.axis_index("ch")

    def over(axis, value, move):
        size = lax.axis_size(axis)
        return lax.ppermute(value, axis, [(p, move(p)) for p in range(size)])

    core, even = gz % 2 == 0, ch % 2 == 0
    here = lambda p: p ^ 1
    there = lambda n: lambda p: (p + (1 if p % 2 else -1)) % n
    layerb = over("gz", jnp.where(core, out_grad[0], out_grad[depth - 1]), there(nz))
    layera = over("gz", jnp.where(core, out_grad[depth - 1], out_grad[0]), here)
    rowb = over("ch", jnp.where(even, inputs[:, 0], inputs[:, rows - 1]), there(ny))
    rowa = over("ch", jnp.where(even, inputs[:, rows - 1], inputs[:, 0]), here)

    wide = jax.ShapeDtypeStruct((blocks * rows, 2 * LANES), BF16)
    e, w, turned = call(
        prep_kernel,
        [
            jax.ShapeDtypeStruct((depth,) + wide.shape, BF16),
            jax.ShapeDtypeStruct((TAPS, TAPS * LANES, 2 * LANES), BF16),
            jax.ShapeDtypeStruct((TAPS * LANES, depth * blocks * rows), BF16),
        ],
        3,
        cost=1 << 29,
    )(out_grad, inputs, filters.T)

    span = blocks * rows
    half = jax.ShapeDtypeStruct((TAPS * chans + chans // 2, LANES), F32)
    edge = jax.ShapeDtypeStruct((depth + 2, width), BF16)
    part, en, r = call(
        functools.partial(own_kernel, chans=chans),
        [
            jax.ShapeDtypeStruct((2,) + half.shape, F32),
            wide,
            jax.ShapeDtypeStruct((span, 4 * LANES), BF16),
        ],
        4,
        cost=1 << 29,
    )(turned, layera, e, out_grad)
    keep, send, vf = call(
        functools.partial(cross_kernel, chans=chans),
        [half, half, jax.ShapeDtypeStruct((TAPS * LANES, span), BF16)],
        5,
        cost=1 << 28,
    )(part, turned, r, rowa, rowb)
    got = over("gz", send, here)
    ef, added = call(functools.partial(far_kernel, chans=chans), [wide, half], 2, cost=1 << 28)(vf, layerb)
    total = keep + got + added
    total, layera, layerb = lax.optimization_barrier((total, layera, layerb))
    first, second = call(edge_kernel, [edge, edge], 3)(out_grad, layera, layerb)

    rounds = []
    for axis, dims in (("gz", [(2 * stride, factor) for stride, factor in steps(nz // 2)]), ("ch", steps(ny))):
        dims = dims[::-1]
        rounds += [(axis, dims)] if [factor for _, factor in dims] == [2, 2] else [(axis, [dim]) for dim in dims]
    recvb = over("ch", second, there(ny))
    recva = over("ch", first, here)
    for number, (axis, dims) in enumerate(rounds):
        count = 1
        for _, factor in dims:
            count *= factor
        values = [total]
        for step in range(1, count):
            values.append(over(axis, total, lambda p: shifted(p, dims, step)))
        for stride, factor in dims:
            groups = [values[k : k + factor] for k in range(0, len(values), factor)]
            if factor > 2:
                digit = lax.axis_index(axis) // stride % factor
                groups = [list(jnp.roll(jnp.stack(group), -digit, axis=0)) for group in groups]
            values = [functools.reduce(lambda x, y: x + y, group) for group in groups]
        total = values[0]
        if number == len(rounds) - 1:
            in_grad = call(grad_kernel, [jax.ShapeDtypeStruct(inputs.shape, BF16)], 6, cost=1 << 30)(
                e, en, ef, w, recva, recvb
            )
            total, in_grad = lax.optimization_barrier((total, in_grad))
    other = over("gz", total, here)
    count = depth * rows * (width // chans) * nz * ny
    scale = float(1.0 / count**0.5)
    filter_grad = call(
        functools.partial(final_kernel, chans=chans, scale=scale), [jax.ShapeDtypeStruct(filters.shape[::-1], F32)], 2
    )(total, other)
    return (in_grad, filter_grad.T)


def solution(mesh):
    placed = (P("gz", "ch", None), P("gz", "ch", None), P())
    return jax.shard_map(
        per_device,
        mesh=mesh,
        in_specs=placed,
        out_specs=(P("gz", "ch", None), P()),
        check_vma=False,
    )
```

```python
import functools

import jax
import jax.numpy as jnp
from jax import lax
from jax.experimental import pallas as pl
from jax.experimental.pallas import tpu as pltpu
from jax.sharding import PartitionSpec as P

LANES = 128
TAPS = 3
ORDER = (0, 2, 1)
F32 = jnp.float32
BF16 = jnp.bfloat16


def windows(layer):
    width = layer.shape[1]
    moved = pltpu.roll(layer, LANES // 2, axis=1)
    tiles = [moved[:, at : at + LANES] for at in range(0, width, LANES)]
    left = jnp.concatenate(tiles, axis=0)
    right = jnp.concatenate(tiles[1:] + tiles[:1], axis=0)
    return jnp.concatenate([left, right], axis=1).astype(BF16)


def stacked(layer):
    return jnp.concatenate(
        [layer[:, at : at + LANES] for at in range(0, layer.shape[1], LANES)], axis=0
    )


def prep_kernel(og_ref, in_ref, f_ref, e_ref, w_ref, t_ref):
    depth, rows = og_ref.shape[:2]
    chans = f_ref.shape[0]
    cells = LANES // chans
    for z in range(depth):
        e_ref[z] = windows(og_ref[z].astype(F32))
    filters = f_ref[...]
    source = lax.broadcasted_iota(jnp.int32, (chans, 2 * LANES), 0)
    target = lax.broadcasted_iota(jnp.int32, (chans, 2 * LANES), 1)
    placed = {}
    for spot in range(1, cells + 3):
        choose = jnp.where(target == source + spot * chans, 1.0, 0.0).astype(BF16)
        placed[spot] = lax.dot_general(
            filters, choose, (((0,), (0,)), ((), ())), preferred_element_type=F32
        )
    for kz in range(TAPS):
        for slot, ky in enumerate(ORDER):
            for b in range(cells):
                total = None
                for kx in range(TAPS):
                    row = ((kz * TAPS + ky) * TAPS + kx) * chans
                    part = placed[b - kx + 3][row : row + chans]
                    total = part if total is None else total + part
                at = slot * LANES + b * chans
                w_ref[kz, at : at + chans] = total.astype(BF16)
    y = lax.broadcasted_iota(jnp.int32, in_ref.shape[1:], 0)
    for ky in range(TAPS):
        shifted = []
        for z in range(depth):
            layer = in_ref[z].astype(F32)
            if ky != 1:
                layer = jnp.where(y == (0 if ky == 0 else rows - 1), 0.0, pltpu.roll(layer, (1 - ky) % rows, axis=0))
            shifted.append(stacked(layer))
        t_ref[ky * LANES : (ky + 1) * LANES] = jnp.concatenate(shifted, axis=0).astype(BF16).T


def diagonal(product, chans):
    cells = LANES // chans
    lane = lax.broadcasted_iota(jnp.int32, (chans, LANES), 1)
    total = product[(cells - 1) * chans :, LANES:]
    for b in range(cells - 1):
        part = product[b * chans : (b + 1) * chans]
        part = jnp.where(lane >= (b + 1) * chans, part[:, :LANES], part[:, LANES:])
        total = total + pltpu.roll(part, LANES - (b + 1) * chans, axis=1)
    return total


def corners():
    return lax.axis_index("gz") % 2 == 0, lax.axis_index("ch") % 2 == 0


def pack(pairs, chans):
    lane = lax.broadcasted_iota(jnp.int32, (chans, LANES), 1)
    valid = TAPS * chans
    halves = []
    for kz, first in ((2, 0), (0, 5)):
        blocks = []
        for ky in range(TAPS):
            source, place = divmod(first + ky, TAPS)
            extra = pairs[1][source]
            if extra is None:
                extra = jnp.zeros((chans, LANES), F32)
            else:
                extra = pltpu.roll(extra, (valid - place * chans) % LANES, axis=1) if place < TAPS else extra
            main = pairs[kz][ky]
            main = jnp.zeros((chans, LANES), F32) if main is None else main
            blocks.append(jnp.where(lane < valid, main, extra))
        tail = jnp.zeros((chans // 2, LANES), F32)
        for number in range(2):
            piece = first + TAPS + number
            if piece >= min(TAPS * TAPS, first + 5):
                continue
            source, place = divmod(piece, TAPS)
            if pairs[1][source] is None:
                continue
            for part in range(2):
                at = number * 2 + part
                value = pairs[1][source][part * chans // 2 : (part + 1) * chans // 2]
                if at != place:
                    value = pltpu.roll(value, (at - place) * chans % LANES, axis=1)
                tail = jnp.where(lane[: chans // 2] // chans == at, value, tail)
        halves.append(jnp.concatenate(blocks + [tail], axis=0))
    return halves


def own_kernel(t_ref, near_ref, e_ref, og_ref, part_ref, en_ref, r_ref, *, chans):
    core, _ = corners()
    depth, rows, width = og_ref.shape
    near = near_ref[...].astype(F32)
    en = windows(near)
    en_ref[...] = en
    zero = jnp.zeros_like(en)
    own = [e_ref[z] for z in range(depth)]
    every = [jnp.where(core, zero, en)] + own + [jnp.where(core, en, zero)]
    pairs = []
    for kz in range(TAPS):
        window = jnp.concatenate(every[2 - kz : 2 - kz + depth], axis=0)
        product = jnp.dot(t_ref[...], window, preferred_element_type=F32)
        pairs.append([diagonal(product[ky * LANES : (ky + 1) * LANES], chans) for ky in range(TAPS)])
    low, high = pack(pairs, chans)
    part_ref[0] = low
    part_ref[1] = high
    layers = [jnp.where(core, 0.0, near)] + [og_ref[z].astype(F32) for z in range(depth)] + [jnp.where(core, near, 0.0)]
    blank = jnp.zeros((depth + 2, width), F32)
    top = jnp.concatenate([layer[0:1] for layer in layers] + [blank], axis=0)
    end = jnp.concatenate([blank] + [layer[rows - 1 : rows] for layer in layers], axis=0)
    r_ref[:, : 2 * LANES] = windows(top)
    r_ref[:, 2 * LANES :] = windows(end)


def cross_kernel(part_ref, t_ref, r_ref, rowa_ref, rowb_ref, keep_ref, send_ref, vf_ref, *, chans):
    core, even = corners()
    depth, width = rowa_ref.shape
    rows = 2 * (depth + 2)
    rowa, rowb = rowa_ref[...].astype(F32), rowb_ref[...].astype(F32)
    lo, hi = jnp.where(even, rowb, rowa), jnp.where(even, rowa, rowb)
    blank = jnp.zeros((2, width), F32)
    base = jnp.concatenate([blank, lo, blank, hi], axis=0)
    left = [stacked(base if kz == 0 else pltpu.roll(base, rows - kz, axis=0)).astype(BF16) for kz in range(TAPS)]
    left = jnp.concatenate(left, axis=1).T
    product = jnp.dot(left, r_ref[...], preferred_element_type=F32)
    pairs = []
    for kz in range(TAPS):
        both = product[kz * LANES : (kz + 1) * LANES]
        pairs.append([diagonal(both[:, : 2 * LANES], chans), None, diagonal(both[:, 2 * LANES :], chans)])
    low, high = pack(pairs, chans)
    low, high = low + part_ref[0], high + part_ref[1]
    keep_ref[...] = jnp.where(core, low, high)
    send_ref[...] = jnp.where(core, high, low)
    y = lax.broadcasted_iota(jnp.int32, (rows, width), 0)
    edge = jnp.where(
        y == 0, jnp.where(core, lo[0:1], lo[depth - 1 : depth]), jnp.where(core, hi[0:1], hi[depth - 1 : depth])
    )
    edge = stacked(edge).astype(BF16).T
    span = edge.shape[1]
    lane = lax.broadcasted_iota(jnp.int32, edge.shape, 1) % rows
    for ky in range(TAPS):
        block = t_ref[ky * LANES : (ky + 1) * LANES]
        value = jnp.where(core, block[:, :span], block[:, (depth - 1) * span :])
        if ky != 1:
            value = jnp.where(lane == (0 if ky == 0 else rows - 1), edge, value)
        vf_ref[ky * LANES : (ky + 1) * LANES] = value


def edge_rows(og_ref, near_ref, far_ref, first_ref, second_ref):
    core, even = corners()
    depth, rows, _ = og_ref.shape
    near, far = near_ref[...].astype(F32), far_ref[...].astype(F32)
    layers = [jnp.where(core, far, near)] + [og_ref[z].astype(F32) for z in range(depth)] + [jnp.where(core, near, far)]
    tops = jnp.concatenate([layer[0:1] for layer in layers], axis=0)
    ends = jnp.concatenate([layer[rows - 1 : rows] for layer in layers], axis=0)
    first_ref[...] = jnp.where(even, ends, tops).astype(BF16)
    second_ref[...] = jnp.where(even, tops, ends).astype(BF16)


def far_kernel(vf_ref, far_ref, og_ref, near_ref, ef_ref, sum_ref, first_ref, second_ref, *, chans):
    window = windows(far_ref[...].astype(F32))
    ef_ref[...] = window
    product = jnp.dot(vf_ref[...], window, preferred_element_type=F32)
    lane = lax.broadcasted_iota(jnp.int32, (chans, LANES), 1)
    for ky in range(TAPS):
        pair = diagonal(product[ky * LANES : (ky + 1) * LANES], chans)
        sum_ref[ky * chans : (ky + 1) * chans] = jnp.where(lane < TAPS * chans, pair, 0.0)
    sum_ref[TAPS * chans :] = jnp.zeros((chans // 2, LANES), F32)
    edge_rows(og_ref, near_ref, far_ref, first_ref, second_ref)


def grad_kernel(e_ref, en_ref, ef_ref, w_ref, rowa_ref, rowb_ref, out_ref):
    depth, rows, width = out_ref.shape
    blocks = width // LANES
    core, even = corners()
    near, far = en_ref[...], ef_ref[...]
    every = [jnp.where(core, far, near)] + [e_ref[z] for z in range(depth)] + [jnp.where(core, near, far)]
    turned = (((1,), (1,)), ((), ()))
    rowa, rowb = rowa_ref[...].astype(F32), rowb_ref[...].astype(F32)
    edges = windows(jnp.concatenate([jnp.where(even, rowb, rowa), jnp.where(even, rowa, rowb)], axis=0))
    layers = depth + 2
    side = None
    for kz in range(TAPS):
        part = lax.dot_general(edges, w_ref[kz, : 2 * LANES], turned, preferred_element_type=F32)
        part = part.reshape(blocks, 2 * layers, 2 * LANES)
        if kz < 2:
            part = pltpu.roll(part, 2 * layers - (2 - kz), axis=1)
        side = part if side is None else side + part
    y = lax.broadcasted_iota(jnp.int32, (blocks, rows, LANES), 1)
    for z in range(depth):
        total = None
        for kz in range(TAPS):
            part = lax.dot_general(every[z - kz + 2], w_ref[kz], turned, preferred_element_type=F32)
            total = part if total is None else total + part
        total = total.reshape(blocks, rows, TAPS * LANES)
        up, down, centre = (total[:, :, slot * LANES : (slot + 1) * LANES] for slot in range(TAPS))
        from_hi = pltpu.roll(side[:, :, :LANES], (rows - 1 - layers - z) % rows, axis=1)
        from_lo = pltpu.roll(side[:, :, LANES:], (rows - z) % rows, axis=1)
        up = jnp.where(y == rows - 1, from_hi, pltpu.roll(up, rows - 1, axis=1))
        down = jnp.where(y == 0, from_lo, pltpu.roll(down, 1, axis=1))
        result = (centre + up + down).astype(BF16)
        for j in range(blocks):
            out_ref[z, :, j * LANES : (j + 1) * LANES] = result[j]


def final_kernel(own_ref, other_ref, out_ref, *, chans, scale):
    core, _ = corners()
    own, other = own_ref[...] * scale, other_ref[...] * scale
    halves = jnp.where(core, own, other), jnp.where(core, other, own)
    for (kz, first), half in zip(((2, 0), (0, 5)), halves):
        turned = half[: TAPS * chans].T
        for ky in range(TAPS):
            block = turned[:, ky * chans : (ky + 1) * chans]
            for kx in range(TAPS):
                place = TAPS - 1 - kx
                at = ((kz * TAPS + ky) * TAPS + kx) * chans
                out_ref[:, at : at + chans] = block[place * chans : (place + 1) * chans]
            source, place = divmod(first + ky, TAPS)
            at = ((TAPS + source) * TAPS + TAPS - 1 - place) * chans
            out_ref[:, at : at + chans] = block[TAPS * chans :]
        tail = half[TAPS * chans :].T
        for number in range(2):
            piece = first + TAPS + number
            if piece >= min(TAPS * TAPS, first + 5):
                continue
            source, place = divmod(piece, TAPS)
            at = ((TAPS + source) * TAPS + TAPS - 1 - place) * chans
            for part in range(2):
                row = (number * 2 + part) * chans
                out_ref[:, at + part * chans // 2 : at + (part + 1) * chans // 2] = tail[row : row + chans]


def call(kernel, outs, n_in, cost=0):
    vmem = pl.BlockSpec(memory_space=pltpu.VMEM)
    single = len(outs) == 1
    return pl.pallas_call(
        kernel,
        out_shape=outs[0] if single else outs,
        in_specs=[vmem] * n_in,
        out_specs=vmem if single else [vmem] * len(outs),
        compiler_params=pltpu.CompilerParams(vmem_limit_bytes=40 * 1024 * 1024),
        cost_estimate=pl.CostEstimate(flops=cost, bytes_accessed=1 << 20, transcendentals=0),
    )


def steps(size):
    stride, found = 1, []
    while size > 1:
        factor = next(f for f in range(2, size + 1) if size % f == 0)
        found.append((stride, factor))
        stride *= factor
        size //= factor
    return found


def shifted(place, dims, step):
    for stride, factor in dims:
        digit = place // stride % factor
        place += ((digit + step % factor) % factor - digit) * stride
        step //= factor
    return place


def per_device(inputs, out_grad, filters):
    depth, rows, width = inputs.shape
    chans = filters.shape[1]
    blocks = width // LANES
    nz, ny = lax.axis_size("gz"), lax.axis_size("ch")
    gz, ch = lax.axis_index("gz"), lax.axis_index("ch")

    def over(axis, value, move):
        size = lax.axis_size(axis)
        return lax.ppermute(value, axis, [(p, move(p)) for p in range(size)])

    core, even = gz % 2 == 0, ch % 2 == 0
    here = lambda p: p ^ 1
    there = lambda n: lambda p: (p + (1 if p % 2 else -1)) % n
    layerb = over("gz", jnp.where(core, out_grad[0], out_grad[depth - 1]), there(nz))
    layera = over("gz", jnp.where(core, out_grad[depth - 1], out_grad[0]), here)
    rowb = over("ch", jnp.where(even, inputs[:, 0], inputs[:, rows - 1]), there(ny))
    rowa = over("ch", jnp.where(even, inputs[:, rows - 1], inputs[:, 0]), here)

    wide = jax.ShapeDtypeStruct((blocks * rows, 2 * LANES), BF16)
    e, w, turned = call(
        prep_kernel,
        [
            jax.ShapeDtypeStruct((depth,) + wide.shape, BF16),
            jax.ShapeDtypeStruct((TAPS, TAPS * LANES, 2 * LANES), BF16),
            jax.ShapeDtypeStruct((TAPS * LANES, depth * blocks * rows), BF16),
        ],
        3,
        cost=1 << 29,
    )(out_grad, inputs, filters.T)

    span = blocks * rows
    half = jax.ShapeDtypeStruct((TAPS * chans + chans // 2, LANES), F32)
    edge = jax.ShapeDtypeStruct((depth + 2, width), BF16)
    part, en, r = call(
        functools.partial(own_kernel, chans=chans),
        [
            jax.ShapeDtypeStruct((2,) + half.shape, F32),
            wide,
            jax.ShapeDtypeStruct((span, 4 * LANES), BF16),
        ],
        4,
        cost=1 << 29,
    )(turned, layera, e, out_grad)
    keep, send, vf = call(
        functools.partial(cross_kernel, chans=chans),
        [half, half, jax.ShapeDtypeStruct((TAPS * LANES, span), BF16)],
        5,
        cost=1 << 28,
    )(part, turned, r, rowa, rowb)
    got = over("gz", send, here)
    ef, added, first, second = call(
        functools.partial(far_kernel, chans=chans), [wide, half, edge, edge], 4, cost=1 << 28
    )(vf, layerb, out_grad, layera)
    total = keep + got + added

    rounds = []
    for axis, dims in (("gz", [(2 * stride, factor) for stride, factor in steps(nz // 2)]), ("ch", steps(ny))):
        dims = dims[::-1]
        rounds += [(axis, dims)] if [factor for _, factor in dims] == [2, 2] else [(axis, [dim]) for dim in dims]
    recvb = over("ch", second, there(ny))
    recva = over("ch", first, here)
    for number, (axis, dims) in enumerate(rounds):
        count = 1
        for _, factor in dims:
            count *= factor
        values = [total]
        for step in range(1, count):
            values.append(over(axis, total, lambda p: shifted(p, dims, step)))
        for stride, factor in dims:
            groups = [values[k : k + factor] for k in range(0, len(values), factor)]
            if factor > 2:
                digit = lax.axis_index(axis) // stride % factor
                groups = [list(jnp.roll(jnp.stack(group), -digit, axis=0)) for group in groups]
            values = [functools.reduce(lambda x, y: x + y, group) for group in groups]
        total = values[0]
        if number == len(rounds) - 1:
            in_grad = call(grad_kernel, [jax.ShapeDtypeStruct(inputs.shape, BF16)], 6, cost=1 << 30)(
                e, en, ef, w, recva, recvb
            )
            total, in_grad = lax.optimization_barrier((total, in_grad))
    other = over("gz", total, here)
    count = depth * rows * (width // chans) * nz * ny
    scale = float(1.0 / count**0.5)
    filter_grad = call(
        functools.partial(final_kernel, chans=chans, scale=scale), [jax.ShapeDtypeStruct(filters.shape[::-1], F32)], 2
    )(total, other)
    return (in_grad, filter_grad.T)


def solution(mesh):
    placed = (P("gz", "ch", None), P("gz", "ch", None), P())
    return jax.shard_map(
        per_device,
        mesh=mesh,
        in_specs=placed,
        out_specs=(P("gz", "ch", None), P()),
        check_vma=False,
    )
```

```python
import functools

import jax
import jax.numpy as jnp
from jax import lax
from jax.experimental import pallas as pl
from jax.experimental.pallas import tpu as pltpu
from jax.sharding import PartitionSpec as P

LANES = 128
TAPS = 3
ORDER = (0, 2, 1)
F32 = jnp.float32
BF16 = jnp.bfloat16


def windows(layer):
    width = layer.shape[1]
    moved = pltpu.roll(layer, LANES // 2, axis=1)
    tiles = [moved[:, at : at + LANES] for at in range(0, width, LANES)]
    left = jnp.concatenate(tiles, axis=0)
    right = jnp.concatenate(tiles[1:] + tiles[:1], axis=0)
    return jnp.concatenate([left, right], axis=1).astype(BF16)


def stacked(layer):
    return jnp.concatenate(
        [layer[:, at : at + LANES] for at in range(0, layer.shape[1], LANES)], axis=0
    )


def prep_kernel(og_ref, in_ref, f_ref, e_ref, w_ref, t_ref):
    depth, rows = og_ref.shape[:2]
    chans = f_ref.shape[0]
    cells = LANES // chans
    for z in range(depth):
        e_ref[z] = windows(og_ref[z].astype(F32))
    filters = f_ref[...]
    source = lax.broadcasted_iota(jnp.int32, (chans, 2 * LANES), 0)
    target = lax.broadcasted_iota(jnp.int32, (chans, 2 * LANES), 1)
    placed = {}
    for spot in range(1, cells + 3):
        choose = jnp.where(target == source + spot * chans, 1.0, 0.0).astype(BF16)
        placed[spot] = lax.dot_general(
            filters, choose, (((0,), (0,)), ((), ())), preferred_element_type=F32
        )
    for kz in range(TAPS):
        for slot, ky in enumerate(ORDER):
            for b in range(cells):
                total = None
                for kx in range(TAPS):
                    row = ((kz * TAPS + ky) * TAPS + kx) * chans
                    part = placed[b - kx + 3][row : row + chans]
                    total = part if total is None else total + part
                at = slot * LANES + b * chans
                w_ref[kz, at : at + chans] = total.astype(BF16)
    y = lax.broadcasted_iota(jnp.int32, in_ref.shape[1:], 0)
    for ky in range(TAPS):
        shifted = []
        for z in range(depth):
            layer = in_ref[z].astype(F32)
            if ky != 1:
                layer = jnp.where(y == (0 if ky == 0 else rows - 1), 0.0, pltpu.roll(layer, (1 - ky) % rows, axis=0))
            shifted.append(stacked(layer))
        t_ref[ky * LANES : (ky + 1) * LANES] = jnp.concatenate(shifted, axis=0).astype(BF16).T


def diagonal(product, chans):
    cells = LANES // chans
    lane = lax.broadcasted_iota(jnp.int32, (chans, LANES), 1)
    total = product[(cells - 1) * chans :, LANES:]
    for b in range(cells - 1):
        part = product[b * chans : (b + 1) * chans]
        part = jnp.where(lane >= (b + 1) * chans, part[:, :LANES], part[:, LANES:])
        total = total + pltpu.roll(part, LANES - (b + 1) * chans, axis=1)
    return total


def corners():
    return lax.axis_index("gz") % 2 == 0, lax.axis_index("ch") % 2 == 0


def pack(pairs, chans):
    lane = lax.broadcasted_iota(jnp.int32, (chans, LANES), 1)
    valid = TAPS * chans
    halves = []
    for kz, first in ((2, 0), (0, 5)):
        blocks = []
        for ky in range(TAPS):
            source, place = divmod(first + ky, TAPS)
            extra = pairs[1][source]
            if extra is None:
                extra = jnp.zeros((chans, LANES), F32)
            else:
                extra = pltpu.roll(extra, (valid - place * chans) % LANES, axis=1) if place < TAPS else extra
            main = pairs[kz][ky]
            main = jnp.zeros((chans, LANES), F32) if main is None else main
            blocks.append(jnp.where(lane < valid, main, extra))
        tail = jnp.zeros((chans // 2, LANES), F32)
        for number in range(2):
            piece = first + TAPS + number
            if piece >= min(TAPS * TAPS, first + 5):
                continue
            source, place = divmod(piece, TAPS)
            if pairs[1][source] is None:
                continue
            for part in range(2):
                at = number * 2 + part
                value = pairs[1][source][part * chans // 2 : (part + 1) * chans // 2]
                if at != place:
                    value = pltpu.roll(value, (at - place) * chans % LANES, axis=1)
                tail = jnp.where(lane[: chans // 2] // chans == at, value, tail)
        halves.append(jnp.concatenate(blocks + [tail], axis=0))
    return halves


def own_kernel(t_ref, near_ref, e_ref, og_ref, part_ref, en_ref, r_ref, *, chans):
    core, _ = corners()
    depth, rows, width = og_ref.shape
    near = near_ref[...].astype(F32)
    en = windows(near)
    en_ref[...] = en
    zero = jnp.zeros_like(en)
    own = [e_ref[z] for z in range(depth)]
    every = [jnp.where(core, zero, en)] + own + [jnp.where(core, en, zero)]
    pairs = []
    for kz in range(TAPS):
        window = jnp.concatenate(every[2 - kz : 2 - kz + depth], axis=0)
        product = jnp.dot(t_ref[...], window, preferred_element_type=F32)
        pairs.append([diagonal(product[ky * LANES : (ky + 1) * LANES], chans) for ky in range(TAPS)])
    low, high = pack(pairs, chans)
    part_ref[0] = low
    part_ref[1] = high
    layers = [jnp.where(core, 0.0, near)] + [og_ref[z].astype(F32) for z in range(depth)] + [jnp.where(core, near, 0.0)]
    blank = jnp.zeros((depth + 2, width), F32)
    top = jnp.concatenate([layer[0:1] for layer in layers] + [blank], axis=0)
    end = jnp.concatenate([blank] + [layer[rows - 1 : rows] for layer in layers], axis=0)
    r_ref[:, : 2 * LANES] = windows(top)
    r_ref[:, 2 * LANES :] = windows(end)


def cross_kernel(part_ref, t_ref, r_ref, rowa_ref, rowb_ref, keep_ref, send_ref, vf_ref, *, chans):
    core, even = corners()
    depth, width = rowa_ref.shape
    rows = 2 * (depth + 2)
    rowa, rowb = rowa_ref[...].astype(F32), rowb_ref[...].astype(F32)
    lo, hi = jnp.where(even, rowb, rowa), jnp.where(even, rowa, rowb)
    blank = jnp.zeros((2, width), F32)
    base = jnp.concatenate([blank, lo, blank, hi], axis=0)
    left = [stacked(base if kz == 0 else pltpu.roll(base, rows - kz, axis=0)).astype(BF16) for kz in range(TAPS)]
    left = jnp.concatenate(left, axis=1).T
    product = jnp.dot(left, r_ref[...], preferred_element_type=F32)
    pairs = []
    for kz in range(TAPS):
        both = product[kz * LANES : (kz + 1) * LANES]
        pairs.append([diagonal(both[:, : 2 * LANES], chans), None, diagonal(both[:, 2 * LANES :], chans)])
    low, high = pack(pairs, chans)
    low, high = low + part_ref[0], high + part_ref[1]
    keep_ref[...] = jnp.where(core, low, high)
    send_ref[...] = jnp.where(core, high, low)
    y = lax.broadcasted_iota(jnp.int32, (rows, width), 0)
    edge = jnp.where(
        y == 0, jnp.where(core, lo[0:1], lo[depth - 1 : depth]), jnp.where(core, hi[0:1], hi[depth - 1 : depth])
    )
    edge = stacked(edge).astype(BF16).T
    span = edge.shape[1]
    lane = lax.broadcasted_iota(jnp.int32, edge.shape, 1) % rows
    for ky in range(TAPS):
        block = t_ref[ky * LANES : (ky + 1) * LANES]
        value = jnp.where(core, block[:, :span], block[:, (depth - 1) * span :])
        if ky != 1:
            value = jnp.where(lane == (0 if ky == 0 else rows - 1), edge, value)
        vf_ref[ky * LANES : (ky + 1) * LANES] = value


def far_kernel(vf_ref, far_ref, ef_ref, sum_ref, *, chans):
    window = windows(far_ref[...].astype(F32))
    ef_ref[...] = window
    product = jnp.dot(vf_ref[...], window, preferred_element_type=F32)
    lane = lax.broadcasted_iota(jnp.int32, (chans, LANES), 1)
    for ky in range(TAPS):
        pair = diagonal(product[ky * LANES : (ky + 1) * LANES], chans)
        sum_ref[ky * chans : (ky + 1) * chans] = jnp.where(lane < TAPS * chans, pair, 0.0)
    sum_ref[TAPS * chans :] = jnp.zeros((chans // 2, LANES), F32)


def edge_kernel(og_ref, near_ref, far_ref, first_ref, second_ref):
    core, even = corners()
    depth, rows, _ = og_ref.shape
    near, far = near_ref[...].astype(F32), far_ref[...].astype(F32)
    layers = [jnp.where(core, far, near)] + [og_ref[z].astype(F32) for z in range(depth)] + [jnp.where(core, near, far)]
    tops = jnp.concatenate([layer[0:1] for layer in layers], axis=0)
    ends = jnp.concatenate([layer[rows - 1 : rows] for layer in layers], axis=0)
    first_ref[...] = jnp.where(even, ends, tops).astype(BF16)
    second_ref[...] = jnp.where(even, tops, ends).astype(BF16)


def grad_kernel(e_ref, en_ref, ef_ref, w_ref, rowa_ref, rowb_ref, out_ref):
    depth, rows, width = out_ref.shape
    blocks = width // LANES
    core, even = corners()
    near, far = en_ref[...], ef_ref[...]
    every = [jnp.where(core, far, near)] + [e_ref[z] for z in range(depth)] + [jnp.where(core, near, far)]
    turned = (((1,), (1,)), ((), ()))
    rowa, rowb = rowa_ref[...].astype(F32), rowb_ref[...].astype(F32)
    edges = windows(jnp.concatenate([jnp.where(even, rowb, rowa), jnp.where(even, rowa, rowb)], axis=0))
    layers = depth + 2
    side = None
    for kz in range(TAPS):
        part = lax.dot_general(edges, w_ref[kz, : 2 * LANES], turned, preferred_element_type=F32)
        part = part.reshape(blocks, 2 * layers, 2 * LANES)
        if kz < 2:
            part = pltpu.roll(part, 2 * layers - (2 - kz), axis=1)
        side = part if side is None else side + part
    y = lax.broadcasted_iota(jnp.int32, (blocks, rows, LANES), 1)
    for z in range(depth):
        total = None
        for kz in range(TAPS):
            part = lax.dot_general(every[z - kz + 2], w_ref[kz], turned, preferred_element_type=F32)
            total = part if total is None else total + part
        total = total.reshape(blocks, rows, TAPS * LANES)
        up, down, centre = (total[:, :, slot * LANES : (slot + 1) * LANES] for slot in range(TAPS))
        from_hi = pltpu.roll(side[:, :, :LANES], (rows - 1 - layers - z) % rows, axis=1)
        from_lo = pltpu.roll(side[:, :, LANES:], (rows - z) % rows, axis=1)
        up = jnp.where(y == rows - 1, from_hi, pltpu.roll(up, rows - 1, axis=1))
        down = jnp.where(y == 0, from_lo, pltpu.roll(down, 1, axis=1))
        result = (centre + up + down).astype(BF16)
        for j in range(blocks):
            out_ref[z, :, j * LANES : (j + 1) * LANES] = result[j]


def final_kernel(own_ref, other_ref, out_ref, *, chans, scale):
    core, _ = corners()
    own, other = own_ref[...] * scale, other_ref[...] * scale
    halves = jnp.where(core, own, other), jnp.where(core, other, own)
    for (kz, first), half in zip(((2, 0), (0, 5)), halves):
        turned = half[: TAPS * chans].T
        for ky in range(TAPS):
            block = turned[:, ky * chans : (ky + 1) * chans]
            for kx in range(TAPS):
                place = TAPS - 1 - kx
                at = ((kz * TAPS + ky) * TAPS + kx) * chans
                out_ref[:, at : at + chans] = block[place * chans : (place + 1) * chans]
            source, place = divmod(first + ky, TAPS)
            at = ((TAPS + source) * TAPS + TAPS - 1 - place) * chans
            out_ref[:, at : at + chans] = block[TAPS * chans :]
        tail = half[TAPS * chans :].T
        for number in range(2):
            piece = first + TAPS + number
            if piece >= min(TAPS * TAPS, first + 5):
                continue
            source, place = divmod(piece, TAPS)
            at = ((TAPS + source) * TAPS + TAPS - 1 - place) * chans
            for part in range(2):
                row = (number * 2 + part) * chans
                out_ref[:, at + part * chans // 2 : at + (part + 1) * chans // 2] = tail[row : row + chans]


def call(kernel, outs, n_in, cost=0):
    vmem = pl.BlockSpec(memory_space=pltpu.VMEM)
    single = len(outs) == 1
    return pl.pallas_call(
        kernel,
        out_shape=outs[0] if single else outs,
        in_specs=[vmem] * n_in,
        out_specs=vmem if single else [vmem] * len(outs),
        compiler_params=pltpu.CompilerParams(vmem_limit_bytes=40 * 1024 * 1024),
        cost_estimate=pl.CostEstimate(flops=cost, bytes_accessed=1 << 20, transcendentals=0),
    )


def steps(size):
    stride, found = 1, []
    while size > 1:
        factor = next(f for f in range(2, size + 1) if size % f == 0)
        found.append((stride, factor))
        stride *= factor
        size //= factor
    return found


def shifted(place, dims, step):
    for stride, factor in dims:
        digit = place // stride % factor
        place += ((digit + step % factor) % factor - digit) * stride
        step //= factor
    return place


def per_device(inputs, out_grad, filters):
    depth, rows, width = inputs.shape
    chans = filters.shape[1]
    blocks = width // LANES
    nz, ny = lax.axis_size("gz"), lax.axis_size("ch")
    gz, ch = lax.axis_index("gz"), lax.axis_index("ch")

    def over(axis, value, move):
        size = lax.axis_size(axis)
        return lax.ppermute(value, axis, [(p, move(p)) for p in range(size)])

    core, even = gz % 2 == 0, ch % 2 == 0
    here = lambda p: p ^ 1
    there = lambda n: lambda p: (p + (1 if p % 2 else -1)) % n
    layerb = over("gz", jnp.where(core, out_grad[0], out_grad[depth - 1]), there(nz))
    layera = over("gz", jnp.where(core, out_grad[depth - 1], out_grad[0]), here)
    rowb = over("ch", jnp.where(even, inputs[:, 0], inputs[:, rows - 1]), there(ny))
    rowa = over("ch", jnp.where(even, inputs[:, rows - 1], inputs[:, 0]), here)

    wide = jax.ShapeDtypeStruct((blocks * rows, 2 * LANES), BF16)
    e, w, turned = call(
        prep_kernel,
        [
            jax.ShapeDtypeStruct((depth,) + wide.shape, BF16),
            jax.ShapeDtypeStruct((TAPS, TAPS * LANES, 2 * LANES), BF16),
            jax.ShapeDtypeStruct((TAPS * LANES, depth * blocks * rows), BF16),
        ],
        3,
        cost=1 << 29,
    )(out_grad, inputs, filters.T)

    span = blocks * rows
    half = jax.ShapeDtypeStruct((TAPS * chans + chans // 2, LANES), F32)
    edge = jax.ShapeDtypeStruct((depth + 2, width), BF16)
    part, en, r = call(
        functools.partial(own_kernel, chans=chans),
        [
            jax.ShapeDtypeStruct((2,) + half.shape, F32),
            wide,
            jax.ShapeDtypeStruct((span, 4 * LANES), BF16),
        ],
        4,
        cost=1 << 29,
    )(turned, layera, e, out_grad)
    keep, send, vf = call(
        functools.partial(cross_kernel, chans=chans),
        [half, half, jax.ShapeDtypeStruct((TAPS * LANES, span), BF16)],
        5,
        cost=1 << 28,
    )(part, turned, r, rowa, rowb)
    got = over("gz", send, here)
    ef, added = call(functools.partial(far_kernel, chans=chans), [wide, half], 2, cost=1 << 28)(vf, layerb)
    total = keep + got + added
    total, layera, layerb = lax.optimization_barrier((total, layera, layerb))
    first, second = call(edge_kernel, [edge, edge], 3)(out_grad, layera, layerb)
    total, first, second = lax.optimization_barrier((total, first, second))

    rounds = []
    for axis, dims in (("gz", [(2 * stride, factor) for stride, factor in steps(nz // 2)]), ("ch", steps(ny))):
        dims = dims[::-1]
        rounds += [(axis, dims)] if [factor for _, factor in dims] == [2, 2] else [(axis, [dim]) for dim in dims]
    recvb = over("ch", second, there(ny))
    recva = over("ch", first, here)
    for number, (axis, dims) in enumerate(rounds):
        count = 1
        for _, factor in dims:
            count *= factor
        values = [total]
        for step in range(1, count):
            values.append(over(axis, total, lambda p: shifted(p, dims, step)))
        for stride, factor in dims:
            groups = [values[k : k + factor] for k in range(0, len(values), factor)]
            if factor > 2:
                digit = lax.axis_index(axis) // stride % factor
                groups = [list(jnp.roll(jnp.stack(group), -digit, axis=0)) for group in groups]
            values = [functools.reduce(lambda x, y: x + y, group) for group in groups]
        total = values[0]
        if number == len(rounds) - 1:
            in_grad = call(grad_kernel, [jax.ShapeDtypeStruct(inputs.shape, BF16)], 6, cost=1 << 30)(
                e, en, ef, w, recva, recvb
            )
            total, in_grad = lax.optimization_barrier((total, in_grad))
    other = over("gz", total, here)
    count = depth * rows * (width // chans) * nz * ny
    scale = float(1.0 / count**0.5)
    filter_grad = call(
        functools.partial(final_kernel, chans=chans, scale=scale), [jax.ShapeDtypeStruct(filters.shape[::-1], F32)], 2
    )(total, other)
    return (in_grad, filter_grad.T)


def solution(mesh):
    placed = (P("gz", "ch", None), P("gz", "ch", None), P())
    return jax.shard_map(
        per_device,
        mesh=mesh,
        in_specs=placed,
        out_specs=(P("gz", "ch", None), P()),
        check_vma=False,
    )
```

```python
import functools

import jax
import jax.numpy as jnp
from jax import lax
from jax.experimental import pallas as pl
from jax.experimental.pallas import tpu as pltpu
from jax.sharding import PartitionSpec as P

LANES = 128
TAPS = 3
ORDER = (0, 2, 1)
F32 = jnp.float32
BF16 = jnp.bfloat16


def windows(layer):
    width = layer.shape[1]
    moved = pltpu.roll(layer, LANES // 2, axis=1)
    tiles = [moved[:, at : at + LANES] for at in range(0, width, LANES)]
    left = jnp.concatenate(tiles, axis=0)
    right = jnp.concatenate(tiles[1:] + tiles[:1], axis=0)
    return jnp.concatenate([left, right], axis=1).astype(BF16)


def stacked(layer):
    return jnp.concatenate(
        [layer[:, at : at + LANES] for at in range(0, layer.shape[1], LANES)], axis=0
    )


def prep_kernel(og_ref, in_ref, f_ref, e_ref, w_ref, t_ref):
    depth, rows = og_ref.shape[:2]
    chans = f_ref.shape[0]
    cells = LANES // chans
    for z in range(depth):
        e_ref[z] = windows(og_ref[z].astype(F32))
    filters = f_ref[...]
    source = lax.broadcasted_iota(jnp.int32, (chans, 2 * LANES), 0)
    target = lax.broadcasted_iota(jnp.int32, (chans, 2 * LANES), 1)
    placed = {}
    for spot in range(1, cells + 3):
        choose = jnp.where(target == source + spot * chans, 1.0, 0.0).astype(BF16)
        placed[spot] = lax.dot_general(
            filters, choose, (((0,), (0,)), ((), ())), preferred_element_type=F32
        )
    for kz in range(TAPS):
        for slot, ky in enumerate(ORDER):
            for b in range(cells):
                total = None
                for kx in range(TAPS):
                    row = ((kz * TAPS + ky) * TAPS + kx) * chans
                    part = placed[b - kx + 3][row : row + chans]
                    total = part if total is None else total + part
                at = slot * LANES + b * chans
                w_ref[kz, at : at + chans] = total.astype(BF16)
    y = lax.broadcasted_iota(jnp.int32, in_ref.shape[1:], 0)
    for ky in range(TAPS):
        shifted = []
        for z in range(depth):
            layer = in_ref[z].astype(F32)
            if ky != 1:
                layer = jnp.where(y == (0 if ky == 0 else rows - 1), 0.0, pltpu.roll(layer, (1 - ky) % rows, axis=0))
            shifted.append(stacked(layer))
        t_ref[ky * LANES : (ky + 1) * LANES] = jnp.concatenate(shifted, axis=0).astype(BF16).T


def diagonal(product, chans):
    cells = LANES // chans
    lane = lax.broadcasted_iota(jnp.int32, (chans, LANES), 1)
    total = product[(cells - 1) * chans :, LANES:]
    for b in range(cells - 1):
        part = product[b * chans : (b + 1) * chans]
        part = jnp.where(lane >= (b + 1) * chans, part[:, :LANES], part[:, LANES:])
        total = total + pltpu.roll(part, LANES - (b + 1) * chans, axis=1)
    return total


def corners():
    return lax.axis_index("gz") % 2 == 0, lax.axis_index("ch") % 2 == 0


def pack(pairs, chans):
    lane = lax.broadcasted_iota(jnp.int32, (chans, LANES), 1)
    valid = TAPS * chans
    halves = []
    for kz, first in ((2, 0), (0, 5)):
        blocks = []
        for ky in range(TAPS):
            source, place = divmod(first + ky, TAPS)
            extra = pairs[1][source]
            if extra is None:
                extra = jnp.zeros((chans, LANES), F32)
            else:
                extra = pltpu.roll(extra, (valid - place * chans) % LANES, axis=1) if place < TAPS else extra
            main = pairs[kz][ky]
            main = jnp.zeros((chans, LANES), F32) if main is None else main
            blocks.append(jnp.where(lane < valid, main, extra))
        tail = jnp.zeros((chans // 2, LANES), F32)
        for number in range(2):
            piece = first + TAPS + number
            if piece >= min(TAPS * TAPS, first + 5):
                continue
            source, place = divmod(piece, TAPS)
            if pairs[1][source] is None:
                continue
            for part in range(2):
                at = number * 2 + part
                value = pairs[1][source][part * chans // 2 : (part + 1) * chans // 2]
                if at != place:
                    value = pltpu.roll(value, (at - place) * chans % LANES, axis=1)
                tail = jnp.where(lane[: chans // 2] // chans == at, value, tail)
        halves.append(jnp.concatenate(blocks + [tail], axis=0))
    return halves


def own_kernel(t_ref, near_ref, e_ref, og_ref, part_ref, en_ref, r_ref, *, chans):
    core, _ = corners()
    depth, rows, width = og_ref.shape
    near = near_ref[...].astype(F32)
    en = windows(near)
    en_ref[...] = en
    zero = jnp.zeros_like(en)
    own = [e_ref[z] for z in range(depth)]
    every = [jnp.where(core, zero, en)] + own + [jnp.where(core, en, zero)]
    pairs = []
    for kz in range(TAPS):
        window = jnp.concatenate(every[2 - kz : 2 - kz + depth], axis=0)
        product = jnp.dot(t_ref[...], window, preferred_element_type=F32)
        pairs.append([diagonal(product[ky * LANES : (ky + 1) * LANES], chans) for ky in range(TAPS)])
    low, high = pack(pairs, chans)
    part_ref[0] = low
    part_ref[1] = high
    layers = [jnp.where(core, 0.0, near)] + [og_ref[z].astype(F32) for z in range(depth)] + [jnp.where(core, near, 0.0)]
    blank = jnp.zeros((depth + 2, width), F32)
    top = jnp.concatenate([layer[0:1] for layer in layers] + [blank], axis=0)
    end = jnp.concatenate([blank] + [layer[rows - 1 : rows] for layer in layers], axis=0)
    r_ref[:, : 2 * LANES] = windows(top)
    r_ref[:, 2 * LANES :] = windows(end)


def cross_kernel(part_ref, t_ref, r_ref, rowa_ref, rowb_ref, keep_ref, send_ref, vf_ref, *, chans):
    core, even = corners()
    depth, width = rowa_ref.shape
    rows = 2 * (depth + 2)
    rowa, rowb = rowa_ref[...].astype(F32), rowb_ref[...].astype(F32)
    lo, hi = jnp.where(even, rowb, rowa), jnp.where(even, rowa, rowb)
    blank = jnp.zeros((2, width), F32)
    base = jnp.concatenate([blank, lo, blank, hi], axis=0)
    left = [stacked(base if kz == 0 else pltpu.roll(base, rows - kz, axis=0)).astype(BF16) for kz in range(TAPS)]
    left = jnp.concatenate(left, axis=1).T
    product = jnp.dot(left, r_ref[...], preferred_element_type=F32)
    pairs = []
    for kz in range(TAPS):
        both = product[kz * LANES : (kz + 1) * LANES]
        pairs.append([diagonal(both[:, : 2 * LANES], chans), None, diagonal(both[:, 2 * LANES :], chans)])
    low, high = pack(pairs, chans)
    low, high = low + part_ref[0], high + part_ref[1]
    keep_ref[...] = jnp.where(core, low, high)
    send_ref[...] = jnp.where(core, high, low)
    y = lax.broadcasted_iota(jnp.int32, (rows, width), 0)
    edge = jnp.where(
        y == 0, jnp.where(core, lo[0:1], lo[depth - 1 : depth]), jnp.where(core, hi[0:1], hi[depth - 1 : depth])
    )
    edge = stacked(edge).astype(BF16).T
    span = edge.shape[1]
    lane = lax.broadcasted_iota(jnp.int32, edge.shape, 1) % rows
    for ky in range(TAPS):
        block = t_ref[ky * LANES : (ky + 1) * LANES]
        value = jnp.where(core, block[:, :span], block[:, (depth - 1) * span :])
        if ky != 1:
            value = jnp.where(lane == (0 if ky == 0 else rows - 1), edge, value)
        vf_ref[ky * LANES : (ky + 1) * LANES] = value


def far_kernel(vf_ref, far_ref, ef_ref, sum_ref, *, chans):
    window = windows(far_ref[...].astype(F32))
    ef_ref[...] = window
    product = jnp.dot(vf_ref[...], window, preferred_element_type=F32)
    lane = lax.broadcasted_iota(jnp.int32, (chans, LANES), 1)
    for ky in range(TAPS):
        pair = diagonal(product[ky * LANES : (ky + 1) * LANES], chans)
        sum_ref[ky * chans : (ky + 1) * chans] = jnp.where(lane < TAPS * chans, pair, 0.0)
    sum_ref[TAPS * chans :] = jnp.zeros((chans // 2, LANES), F32)


def edge_kernel(og_ref, near_ref, far_ref, first_ref, second_ref):
    core, even = corners()
    depth, rows, _ = og_ref.shape
    near, far = near_ref[...].astype(F32), far_ref[...].astype(F32)
    layers = [jnp.where(core, far, near)] + [og_ref[z].astype(F32) for z in range(depth)] + [jnp.where(core, near, far)]
    tops = jnp.concatenate([layer[0:1] for layer in layers], axis=0)
    ends = jnp.concatenate([layer[rows - 1 : rows] for layer in layers], axis=0)
    first_ref[...] = jnp.where(even, ends, tops).astype(BF16)
    second_ref[...] = jnp.where(even, tops, ends).astype(BF16)


def grad_kernel(e_ref, en_ref, ef_ref, w_ref, rowa_ref, rowb_ref, out_ref):
    depth, rows, width = out_ref.shape
    blocks = width // LANES
    core, even = corners()
    near, far = en_ref[...], ef_ref[...]
    every = [jnp.where(core, far, near)] + [e_ref[z] for z in range(depth)] + [jnp.where(core, near, far)]
    turned = (((1,), (1,)), ((), ()))
    rowa, rowb = rowa_ref[...].astype(F32), rowb_ref[...].astype(F32)
    edges = windows(jnp.concatenate([jnp.where(even, rowb, rowa), jnp.where(even, rowa, rowb)], axis=0))
    layers = depth + 2
    side = None
    for kz in range(TAPS):
        part = lax.dot_general(edges, w_ref[kz, : 2 * LANES], turned, preferred_element_type=F32)
        part = part.reshape(blocks, 2 * layers, 2 * LANES)
        if kz < 2:
            part = pltpu.roll(part, 2 * layers - (2 - kz), axis=1)
        side = part if side is None else side + part
    y = lax.broadcasted_iota(jnp.int32, (blocks, rows, LANES), 1)
    for z in range(depth):
        total = None
        for kz in range(TAPS):
            part = lax.dot_general(every[z - kz + 2], w_ref[kz], turned, preferred_element_type=F32)
            total = part if total is None else total + part
        total = total.reshape(blocks, rows, TAPS * LANES)
        up, down, centre = (total[:, :, slot * LANES : (slot + 1) * LANES] for slot in range(TAPS))
        from_hi = pltpu.roll(side[:, :, :LANES], (rows - 1 - layers - z) % rows, axis=1)
        from_lo = pltpu.roll(side[:, :, LANES:], (rows - z) % rows, axis=1)
        up = jnp.where(y == rows - 1, from_hi, pltpu.roll(up, rows - 1, axis=1))
        down = jnp.where(y == 0, from_lo, pltpu.roll(down, 1, axis=1))
        result = (centre + up + down).astype(BF16)
        for j in range(blocks):
            out_ref[z, :, j * LANES : (j + 1) * LANES] = result[j]


def final_kernel(own_ref, other_ref, out_ref, *, chans, scale):
    core, _ = corners()
    own, other = own_ref[...] * scale, other_ref[...] * scale
    halves = jnp.where(core, own, other), jnp.where(core, other, own)
    for (kz, first), half in zip(((2, 0), (0, 5)), halves):
        turned = half[: TAPS * chans].T
        for ky in range(TAPS):
            block = turned[:, ky * chans : (ky + 1) * chans]
            for kx in range(TAPS):
                place = TAPS - 1 - kx
                at = ((kz * TAPS + ky) * TAPS + kx) * chans
                out_ref[:, at : at + chans] = block[place * chans : (place + 1) * chans]
            source, place = divmod(first + ky, TAPS)
            at = ((TAPS + source) * TAPS + TAPS - 1 - place) * chans
            out_ref[:, at : at + chans] = block[TAPS * chans :]
        tail = half[TAPS * chans :].T
        for number in range(2):
            piece = first + TAPS + number
            if piece >= min(TAPS * TAPS, first + 5):
                continue
            source, place = divmod(piece, TAPS)
            at = ((TAPS + source) * TAPS + TAPS - 1 - place) * chans
            for part in range(2):
                row = (number * 2 + part) * chans
                out_ref[:, at + part * chans // 2 : at + (part + 1) * chans // 2] = tail[row : row + chans]


def call(kernel, outs, n_in, cost=0):
    vmem = pl.BlockSpec(memory_space=pltpu.VMEM)
    single = len(outs) == 1
    return pl.pallas_call(
        kernel,
        out_shape=outs[0] if single else outs,
        in_specs=[vmem] * n_in,
        out_specs=vmem if single else [vmem] * len(outs),
        compiler_params=pltpu.CompilerParams(vmem_limit_bytes=24 * 1024 * 1024),
        cost_estimate=pl.CostEstimate(flops=cost, bytes_accessed=1 << 20, transcendentals=0),
    )


def steps(size):
    stride, found = 1, []
    while size > 1:
        factor = next(f for f in range(2, size + 1) if size % f == 0)
        found.append((stride, factor))
        stride *= factor
        size //= factor
    return found


def shifted(place, dims, step):
    for stride, factor in dims:
        digit = place // stride % factor
        place += ((digit + step % factor) % factor - digit) * stride
        step //= factor
    return place


def per_device(inputs, out_grad, filters):
    depth, rows, width = inputs.shape
    chans = filters.shape[1]
    blocks = width // LANES
    nz, ny = lax.axis_size("gz"), lax.axis_size("ch")
    gz, ch = lax.axis_index("gz"), lax.axis_index("ch")

    def over(axis, value, move):
        size = lax.axis_size(axis)
        return lax.ppermute(value, axis, [(p, move(p)) for p in range(size)])

    core, even = gz % 2 == 0, ch % 2 == 0
    here = lambda p: p ^ 1
    there = lambda n: lambda p: (p + (1 if p % 2 else -1)) % n
    layerb = over("gz", jnp.where(core, out_grad[0], out_grad[depth - 1]), there(nz))
    layera = over("gz", jnp.where(core, out_grad[depth - 1], out_grad[0]), here)
    rowb = over("ch", jnp.where(even, inputs[:, 0], inputs[:, rows - 1]), there(ny))
    rowa = over("ch", jnp.where(even, inputs[:, rows - 1], inputs[:, 0]), here)

    wide = jax.ShapeDtypeStruct((blocks * rows, 2 * LANES), BF16)
    e, w, turned = call(
        prep_kernel,
        [
            jax.ShapeDtypeStruct((depth,) + wide.shape, BF16),
            jax.ShapeDtypeStruct((TAPS, TAPS * LANES, 2 * LANES), BF16),
            jax.ShapeDtypeStruct((TAPS * LANES, depth * blocks * rows), BF16),
        ],
        3,
        cost=1 << 29,
    )(out_grad, inputs, filters.T)

    span = blocks * rows
    half = jax.ShapeDtypeStruct((TAPS * chans + chans // 2, LANES), F32)
    edge = jax.ShapeDtypeStruct((depth + 2, width), BF16)
    part, en, r = call(
        functools.partial(own_kernel, chans=chans),
        [
            jax.ShapeDtypeStruct((2,) + half.shape, F32),
            wide,
            jax.ShapeDtypeStruct((span, 4 * LANES), BF16),
        ],
        4,
        cost=1 << 29,
    )(turned, layera, e, out_grad)
    keep, send, vf = call(
        functools.partial(cross_kernel, chans=chans),
        [half, half, jax.ShapeDtypeStruct((TAPS * LANES, span), BF16)],
        5,
        cost=1 << 28,
    )(part, turned, r, rowa, rowb)
    got = over("gz", send, here)
    ef, added = call(functools.partial(far_kernel, chans=chans), [wide, half], 2, cost=1 << 28)(vf, layerb)
    total = keep + got + added
    total, layera, layerb = lax.optimization_barrier((total, layera, layerb))
    first, second = call(edge_kernel, [edge, edge], 3)(out_grad, layera, layerb)

    rounds = []
    for axis, dims in (("gz", [(2 * stride, factor) for stride, factor in steps(nz // 2)]), ("ch", steps(ny))):
        dims = dims[::-1]
        rounds += [(axis, dims)] if [factor for _, factor in dims] == [2, 2] else [(axis, [dim]) for dim in dims]
    recvb = over("ch", second, there(ny))
    recva = over("ch", first, here)
    for number, (axis, dims) in enumerate(rounds):
        count = 1
        for _, factor in dims:
            count *= factor
        values = [total]
        for step in range(1, count):
            values.append(over(axis, total, lambda p: shifted(p, dims, step)))
        for stride, factor in dims:
            groups = [values[k : k + factor] for k in range(0, len(values), factor)]
            if factor > 2:
                digit = lax.axis_index(axis) // stride % factor
                groups = [list(jnp.roll(jnp.stack(group), -digit, axis=0)) for group in groups]
            values = [functools.reduce(lambda x, y: x + y, group) for group in groups]
        total = values[0]
        if number == len(rounds) - 1:
            in_grad = call(grad_kernel, [jax.ShapeDtypeStruct(inputs.shape, BF16)], 6, cost=1 << 30)(
                e, en, ef, w, recva, recvb
            )
            total, in_grad = lax.optimization_barrier((total, in_grad))
    other = over("gz", total, here)
    count = depth * rows * (width // chans) * nz * ny
    scale = float(1.0 / count**0.5)
    filter_grad = call(
        functools.partial(final_kernel, chans=chans, scale=scale), [jax.ShapeDtypeStruct(filters.shape[::-1], F32)], 2
    )(total, other)
    return (in_grad, filter_grad.T)


def solution(mesh):
    placed = (P("gz", "ch", None), P("gz", "ch", None), P())
    return jax.shard_map(
        per_device,
        mesh=mesh,
        in_specs=placed,
        out_specs=(P("gz", "ch", None), P()),
        check_vma=False,
    )
```
